256 devices in a mesh: dp: 16 (over z_hi, x, core), fsdp: 16 (over z_lo, y).
Axes of the slice: x: 4, y: 4, z: 8 (z_hi: 2, z_lo: 4; z = z_hi * 4 + z_lo), core: 2. Of those that a mesh axis runs over, the one named last changes fastest.
Arguments:
- vlm_rows: bfloat16 [256, 32, 7168], P(('dp', 'fsdp')), may hold values from -300 to 300
- images: int32 [256], P(('dp', 'fsdp')), may hold values from 1 to 2
- action_hidden: bfloat16 [256, 128, 1536], P(('dp', 'fsdp')), may hold values from -1000 to 1000
- lengths: int32 [256], P(('dp', 'fsdp')), may hold values from 1 to 16
- vlm_weight: bfloat16 [7168, 7168], P('dp', 'fsdp'), may hold values from -0.0625 to 0.0625
- kv_weight: bfloat16 [3072, 7168], P('fsdp', 'dp'), may hold values from -0.0625 to 0.0625
- query_weight: bfloat16 [1536, 1536], replicated, may hold values from -0.15625 to 0.15625
- context_grad: bfloat16 [256, 128, 1536], P(('dp', 'fsdp')), may hold values from -0.75 to 0.75
Outputs:
- context: bfloat16 [256, 128, 1536], P(('dp', 'fsdp'))
- kv_weight_grad: float32 [3072, 7168], P('fsdp', 'dp')
The draws below stay inside these ranges and needn't reach their ends.
Inputs may be any that keep to these rules, and one draw needn't show every extreme that they name: Rows r of sample s with r < 16 * images[s] hold image tokens, the others are padding.
All inputs are finite; a program needn't handle non-finite values.
Results may differ from the reference program's by a relative error of at most 0.025.
The reference program's roundings to bfloat16 on the way (of `normed`, `feature`, `kv_rows`, `queries`, `probs_low`, `grad_in`, `score_grad` and `kv_grads`) count: a program that leaves them out, or rounds other values in their place, can miss the bound.
Values may be sent and summed in bfloat16 or wider, within the bound.
No kernel may reach another device: no remote copies, remote signals or barrier semaphores. Data moves between devices by JAX's collectives and lax.ppermute only.
A program may use at most 64 MiB of HBM per device.

```python
import jax
import jax.numpy as jnp
from jax import lax

DV = 7168
DA = 1536
HEAD_DIM = 48
IMG_TOK = 16
MAX_IMG = 2
ACT = 16
VROWS = 32
QROWS = 128
SAMPLES = 256


def draw_vlm_rows(key, part):
    key = jax.random.fold_in(key, 7)
    key_base = jax.random.fold_in(key, 0)
    values = jax.random.truncated_normal(key_base, -5.0, 5.0, (SAMPLES, VROWS, DV), jnp.float32)
    return jnp.clip(values, -300.0, 300.0).astype(jnp.bfloat16)


def draw_action_hidden(key, part):
    key = jax.random.fold_in(key, 13)
    key_base = jax.random.fold_in(key, 0)
    values = jax.random.truncated_normal(key_base, -5.0, 5.0, (SAMPLES, QROWS, DA), jnp.float32)
    return jnp.clip(values, -1000.0, 1000.0).astype(jnp.bfloat16)


def plant(drawn, stream_key, least, largest):
    dims = drawn.shape
    index_at = [jax.random.randint(jax.random.fold_in(stream_key, axis), (), 0, dims[axis]) for axis in range(len(dims))]
    drawn = drawn.at[tuple(index_at)].set(least)
    longest = dims.index(max(dims))
    index_at[longest] = (index_at[longest] + 1) % dims[longest]
    return drawn.at[tuple(index_at)].set(largest)


def with_spikes(entries, stream_key, source, target, parts, factor):
    def block_of(axis_at):
        return (jnp.arange(entries.shape[axis_at]) // (entries.shape[axis_at] // parts)).reshape((-1,) + (1,) * (entries.ndim - 1 - axis_at))

    near = jax.random.permutation(stream_key, parts)[block_of(target)]
    second = (block_of(target) + parts // 2) % parts
    return jnp.where((block_of(source) == near) | (block_of(source) == second), factor * entries, entries)


def shard_levels(rng, shape, cuts, smallest, largest):
    def one(position, blocks):
        steps = jax.random.uniform(jax.random.fold_in(jax.random.fold_in(rng, 6), position), (blocks,), jnp.float32, smallest / len(cuts), largest / len(cuts))
        return jnp.repeat(jnp.exp(steps), shape[position] // blocks).reshape((-1,) + (1,) * (len(shape) - position - 1))

    factor_of = one(*cuts[0])
    for cut in cuts[1:]:
        factor_of = factor_of * one(*cut)
    return factor_of


def bell_draw(key, dims, deviation, most, cuts=(), kind=jnp.bfloat16):
    drawn = jax.random.normal(key, dims, jnp.float32) * deviation
    if len(cuts) > 0:
        drawn = shard_levels(key, dims, cuts, -0.22, 0.18) * drawn
    return jnp.clip(drawn, min=-most, max=most).astype(kind)


def gaussian_with(key, dims, scale, most, shards, heavy, kind=jnp.bfloat16):
    array = scale * jax.random.normal(key, dims, jnp.float32)
    if shards:
        array = array * shard_levels(key, dims, shards, -0.22, 0.18)
    return jnp.clip(with_spikes(array, jax.random.fold_in(key, 3), *heavy), -most, most).astype(kind)


def setup_inputs(seed: int = 0) -> dict:
    seeds = jax.random.split(jax.random.key(seed), 9)
    vlm_rows = draw_vlm_rows(jax.random.fold_in(seeds[8], 71), 0)
    images = plant(jax.random.randint(seeds[1], (SAMPLES,), 1, MAX_IMG + 1), jax.random.fold_in(seeds[1], 1), 1, MAX_IMG).astype(jnp.int32)
    action_hidden = draw_action_hidden(jax.random.fold_in(seeds[8], 71), 0)
    lengths = plant(jax.random.randint(seeds[3], (SAMPLES,), 1, ACT + 1), jax.random.fold_in(seeds[3], 1), 1, ACT).astype(jnp.int32)
    vlm_weight = bell_draw(seeds[4], (DV, DV), DV ** -0.5, 0.0625, ((0, 16), (1, 16)))
    kv_weight = bell_draw(seeds[5], (2 * DA, DV), DV ** -0.5, 0.0625, ((0, 16), (1, 16)))
    query_weight = bell_draw(seeds[6], (DA, DA), DA ** -0.5, 0.15625)
    context_grad = gaussian_with(seeds[7], (SAMPLES, QROWS, DA), 0.03, 0.75, ((0, 256),), (0, 2, 256, 6.0))
    return dict(vlm_rows=vlm_rows, images=images, action_hidden=action_hidden, lengths=lengths, vlm_weight=vlm_weight, kv_weight=kv_weight, query_weight=query_weight, context_grad=context_grad)


eps = 1e-06
masked_value = -1e+30

def cross_attention(kv_rows, queries, images, lengths, context_grad):
    samples, qrows, width_act = queries.shape
    heads = width_act // HEAD_DIM
    softmax_scale = HEAD_DIM ** (-0.5)
    keys = kv_rows[:, :width_act].reshape(samples, -1, heads, HEAD_DIM).astype(jnp.float32)
    values = kv_rows[:, width_act:].reshape(samples, -1, heads, HEAD_DIM).astype(jnp.float32)
    query_heads = queries.reshape(samples, qrows, heads, HEAD_DIM).astype(jnp.float32)
    scores = jnp.einsum('sqhd,skhd->shqk', query_heads, keys) * softmax_scale
    key_rows = keys.shape[1]
    key_live = jnp.arange(key_rows, dtype=jnp.int32)[None, :] < images[:, None] * IMG_TOK
    scores = jnp.where(key_live[:, None, None, :], scores, masked_value)
    row_peak = lax.optimization_barrier(jnp.max(scores, axis=-1, keepdims=True))
    exponent = jnp.exp(scores - row_peak)
    probs = exponent / lax.optimization_barrier(jnp.sum(exponent, axis=-1, keepdims=True))
    probs_low = probs.astype(jnp.bfloat16).astype(jnp.float32)
    query_live = (jnp.arange(qrows, dtype=jnp.int32) % ACT)[None, :] < lengths[:, None]
    mixed_heads = jnp.einsum('shqk,skhd->sqhd', probs_low, values)
    context = jnp.where(query_live[:, :, None, None], mixed_heads, 0.0).astype(jnp.bfloat16)
    context = context.reshape(samples, qrows, width_act)
    grad_in = jnp.where(query_live[:, :, None], context_grad, jnp.zeros_like(context_grad))
    grad_in = grad_in.reshape(samples, qrows, heads, HEAD_DIM).astype(jnp.float32)
    value_grad = jnp.einsum('shqk,sqhd->skhd', probs_low, grad_in)
    prob_grad = jnp.einsum('sqhd,skhd->shqk', grad_in, values)
    centre = lax.optimization_barrier(jnp.sum(prob_grad * probs, axis=-1, keepdims=True))
    score_grad = (probs * (prob_grad - centre)).astype(jnp.bfloat16).astype(jnp.float32)
    key_grad = jnp.einsum('shqk,sqhd->skhd', score_grad, query_heads) * softmax_scale
    kv_grads = jnp.concatenate([key_grad.reshape(-1, width_act), value_grad.reshape(-1, width_act)], axis=1)
    return (context, kv_grads.astype(jnp.bfloat16))

def reference(vlm_rows, images, action_hidden, lengths, vlm_weight, kv_weight, query_weight, context_grad):
    flat_rows = vlm_rows.reshape(-1, DV)
    widened = flat_rows.astype(jnp.float32)
    normed = (widened * lax.rsqrt(lax.optimization_barrier(jnp.mean(widened * widened, axis=-1, keepdims=True)) + eps)).astype(jnp.bfloat16)
    pre_act = lax.dot_general(normed, vlm_weight, (((1,), (1,)), ((), ())), preferred_element_type=jnp.float32)
    feature = (widened + jax.nn.silu(pre_act)).astype(jnp.bfloat16)
    kv_total = lax.dot_general(feature, kv_weight, (((1,), (1,)), ((), ())), preferred_element_type=jnp.float32)
    kv_rows = kv_total.astype(jnp.bfloat16)
    queries = lax.dot_general(action_hidden.reshape(-1, DA), query_weight, (((1,), (1,)), ((), ())), preferred_element_type=jnp.float32)
    queries = queries.astype(jnp.bfloat16).reshape(action_hidden.shape)
    context, kv_grads = cross_attention(kv_rows, queries, images, lengths, context_grad)
    kv_weight_grad = lax.dot_general(kv_grads, feature, (((0,), (0,)), ((), ())), preferred_element_type=jnp.float32)
    return (context, kv_weight_grad)
```

```python
import jax
import jax.numpy as jnp
from jax import lax
from jax.experimental import pallas as pl
from jax.experimental.pallas import tpu as pltpu
from jax.sharding import PartitionSpec as P

HEAD_DIM = 48
IMG_TOK = 16
ACT = 16
AXES = ("dp", "fsdp")

eps = 1e-06
masked_value = -1e30
bf16 = jnp.bfloat16
f32 = jnp.float32
VMEM_BYTES = 56 * 1024 * 1024


def pairs(step):
    table = []
    for i in range(256):
        h, x, c, l, y = step(i >> 7, (i >> 5) & 3, (i >> 4) & 1, (i >> 2) & 3, i & 3)
        table.append((i, h << 7 | x << 5 | c << 4 | l << 2 | y))
    return table


CORE = pairs(lambda h, x, c, l, y: (h, x, c ^ 1, l, y))
MIRROR = pairs(lambda h, x, c, l, y: (h ^ 1, x, c, l ^ 3, y))
HALF = pairs(lambda h, x, c, l, y: (h ^ 1, x, c, l, y))
ALONG_X = [pairs(lambda h, x, c, l, y, e=e: (h, x ^ e, c, l, y)) for e in range(4)]


def send(array, table):
    return lax.ppermute(array, AXES, table)


def gather_group(own, partner):
    both = jnp.stack([own, send(own, partner)])
    return jnp.concatenate([both] + [send(both, ALONG_X[e]) for e in (1, 2, 3)], axis=0)


def norm_kernel(col_ref, rows_ref, normed_ref, resid_ref):
    widened = rows_ref[0].astype(f32)
    mean = jnp.mean(widened * widened, axis=-1, keepdims=True)
    normed = (widened * lax.rsqrt(mean + eps)).astype(bf16)
    blocks, _, depth = normed_ref.shape
    for f in range(blocks):
        normed_ref[f] = normed[:, f * depth : (f + 1) * depth]

        @pl.when(col_ref[0] == f)
        def _():
            resid_ref[...] = rows_ref[0, :, f * depth : (f + 1) * depth]


def normalize(rows, col):
    slots, height, width = rows.shape
    depth = width // 16
    return pl.pallas_call(
        norm_kernel,
        grid=(slots,),
        in_specs=[
            pl.BlockSpec(memory_space=pltpu.SMEM),
            pl.BlockSpec((1, height, width), lambda i: (i, 0, 0)),
        ],
        out_specs=[
            pl.BlockSpec((16, height, depth), lambda i: (0, i, 0)),
            pl.BlockSpec((height, depth), lambda i: (i, 0)),
        ],
        out_shape=[
            jax.ShapeDtypeStruct((16, slots * height, depth), bf16),
            jax.ShapeDtypeStruct((slots * height, depth), bf16),
        ],
        compiler_params=pltpu.CompilerParams(vmem_limit_bytes=VMEM_BYTES),
        name="norm",
    )(col, rows)


def layer_kernel(na_ref, nb_ref, ra_ref, rb_ref, w_ref, featt_ref, pa_ref, pb_ref, acc, kvw):
    k = pl.program_id(0)
    half = na_ref.shape[1]
    out = ra_ref.shape[1]
    kv = w_ref.shape[2] - out

    @pl.when(k == 0)
    def _():
        acc[...] = jnp.zeros_like(acc)

    w = w_ref[0, :, :out]
    acc[:half] += jnp.dot(na_ref[0], w, preferred_element_type=f32)
    acc[half:] += jnp.dot(nb_ref[0], w, preferred_element_type=f32)
    for odd in range(2):

        @pl.when(k % 2 == odd)
        def _():
            kvw[k // 2, :, odd * kv : (odd + 1) * kv] = w_ref[0, :, out:]

    @pl.when(k == pl.num_programs(0) - 1)
    def _():
        for lo, r_ref, p_ref in ((0, ra_ref, pa_ref), (half, rb_ref, pb_ref)):
            pre = acc[lo : lo + half]
            feature = (r_ref[...].astype(f32) + pre / (1.0 + jnp.exp(-pre))).astype(bf16)
            featt_ref[:, lo : lo + half] = feature.T
            for j in range(kvw.shape[0]):
                p_ref[:, j * 2 * kv : (j + 1) * 2 * kv] = jnp.dot(
                    feature, kvw[j], preferred_element_type=f32
                ).astype(p_ref.dtype)


def layer(na, nb, ra, rb, weights):
    blocks, half, depth = na.shape
    out = ra.shape[1]
    kv = weights.shape[2] - out
    row_block = pl.BlockSpec((1, half, depth), lambda k: (k, 0, 0))

    def whole(shape):
        return pl.BlockSpec(shape, lambda k: (0, 0))

    return pl.pallas_call(
        layer_kernel,
        grid=(blocks,),
        in_specs=[
            row_block,
            row_block,
            whole(ra.shape),
            whole(rb.shape),
            pl.BlockSpec((1, depth, out + kv), lambda k: (k, 0, 0)),
        ],
        out_specs=[whole((out, 2 * half)), whole((half, blocks * kv)), whole((half, blocks * kv))],
        out_shape=[
            jax.ShapeDtypeStruct((out, 2 * half), bf16),
            jax.ShapeDtypeStruct((half, blocks * kv), f32),
            jax.ShapeDtypeStruct((half, blocks * kv), bf16),
        ],
        scratch_shapes=[
            pltpu.VMEM((2 * half, out), f32),
            pltpu.VMEM((blocks // 2, depth, 2 * kv), bf16),
        ],
        compiler_params=pltpu.CompilerParams(vmem_limit_bytes=VMEM_BYTES),
        name="layer",
    )(na, nb, ra, rb, weights)


def attention_kernel(
    images_ref, lengths_ref, own_ref, other_ref, q_ref, cg_ref, context_ref, grads_ref
):
    key_rows, width = own_ref.shape
    width_act = width // 2
    qrows = q_ref.shape[0]
    heads = 8
    cols = heads * HEAD_DIM
    scale = HEAD_DIM ** (-0.5)
    piece = grads_ref.shape[2]
    last = (((1,), (1,)), ((), ()))
    first = (((0,), (0,)), ((), ()))
    kv = (own_ref[...] + other_ref[...].astype(f32)).astype(bf16)
    row_head = lax.broadcasted_iota(jnp.int32, (heads * key_rows, cols), 0) // key_rows
    col_head = lax.broadcasted_iota(jnp.int32, (heads * key_rows, cols), 1) // HEAD_DIM
    same = row_head == col_head
    key_live = (
        lax.broadcasted_iota(jnp.int32, (heads, key_rows, qrows), 1) < images_ref[0] * IMG_TOK
    )
    query_live = lax.broadcasted_iota(jnp.int32, (qrows, cols), 0) % ACT < lengths_ref[0]

    def by_head(flat):
        return flat.reshape(heads, key_rows, qrows)

    def spread(rows):
        return jnp.where(same, jnp.concatenate([rows] * heads, axis=0), jnp.zeros((), bf16))

    def collapse(big):
        return jnp.sum(jnp.where(same, big, 0.0).reshape(heads, key_rows, cols), axis=0)

    for g in range(width_act // cols):
        at = slice(g * cols, (g + 1) * cols)
        keys = spread(kv[:, g * cols : (g + 1) * cols])
        values = spread(kv[:, width_act + g * cols : width_act + (g + 1) * cols])
        queries = q_ref[:, at]
        grad_in = jnp.where(query_live, cg_ref[:, at], jnp.zeros((), bf16))
        scores = by_head(lax.dot_general(keys, queries, last, preferred_element_type=f32) * scale)
        scores = jnp.where(key_live, scores, masked_value)
        exponent = jnp.exp(scores - jnp.max(scores, axis=1, keepdims=True))
        probs = exponent / jnp.sum(exponent, axis=1, keepdims=True)
        probs_low = probs.astype(bf16).reshape(heads * key_rows, qrows)
        mixed = lax.dot_general(probs_low, values, first, preferred_element_type=f32)
        context_ref[:, at] = jnp.where(query_live, mixed, 0.0).astype(bf16)
        prob_grad = by_head(lax.dot_general(values, grad_in, last, preferred_element_type=f32))
        centre = jnp.sum(prob_grad * probs, axis=1, keepdims=True)
        score_grad = (probs * (prob_grad - centre)).astype(bf16).reshape(heads * key_rows, qrows)
        value_grad = collapse(jnp.dot(probs_low, grad_in, preferred_element_type=f32)).astype(bf16)
        key_grad = jnp.dot(score_grad, queries, preferred_element_type=f32)
        key_grad = (collapse(key_grad) * scale).astype(bf16)
        per = cols // piece
        for start, grad in ((g * per, key_grad), (width_act // piece + g * per, value_grad)):
            for j in range(per):
                grads_ref[start + j] = grad[:, j * piece : (j + 1) * piece]


def attention(own, other, queries, images, lengths, context_grad):
    key_rows, width = own.shape
    smem, vmem = pl.BlockSpec(memory_space=pltpu.SMEM), pl.BlockSpec(memory_space=pltpu.VMEM)
    return pl.pallas_call(
        attention_kernel,
        in_specs=[smem, smem, vmem, vmem, vmem, vmem],
        out_specs=[vmem, vmem],
        out_shape=[
            jax.ShapeDtypeStruct(queries.shape, bf16),
            jax.ShapeDtypeStruct((16, key_rows, width // 16), bf16),
        ],
        compiler_params=pltpu.CompilerParams(vmem_limit_bytes=VMEM_BYTES),
        name="attention",
    )(images, lengths, own, other, queries, context_grad)


def weight_grad_kernel(a0_ref, a1_ref, b0_ref, b1_ref, featt_ref, out_ref, acc):
    f = pl.program_id(0)
    kv = out_ref.shape[0]

    @pl.when(f == 0)
    def _():
        acc[...] = jnp.zeros_like(acc)

    def rows(first_ref, second_ref):
        return jnp.stack([first_ref[:, 0, 0], second_ref[:, 0, 0]], axis=1).reshape(-1, kv)

    grads = jnp.concatenate([rows(a0_ref, a1_ref), rows(b0_ref, b1_ref)], axis=0)
    acc[...] += jnp.dot(featt_ref[0], grads, preferred_element_type=f32)

    @pl.when(f == pl.num_programs(0) - 1)
    def _():
        out_ref[...] = acc[...].T


def weight_grad(grads_a, grads_b, featt):
    blocks, out, rows = featt.shape
    slots, _, key_rows, kv = grads_a.shape
    grads_a = grads_a.reshape(slots // 2, 2, blocks, key_rows, kv)
    grads_b = grads_b.reshape(slots // 2, 2, blocks, key_rows, kv)
    block = (slots // 2, 1, 1, key_rows, kv)
    near = pl.BlockSpec(block, lambda f: (0, 0, f, 0, 0))
    far = pl.BlockSpec(block, lambda f: (0, 1, 12 - (f // 4) * 4 + f % 4, 0, 0))
    return pl.pallas_call(
        weight_grad_kernel,
        grid=(blocks,),
        in_specs=[near, far, near, far, pl.BlockSpec((1, out, rows), lambda f: (f, 0, 0))],
        out_specs=pl.BlockSpec((kv, out), lambda f: (0, 0)),
        out_shape=jax.ShapeDtypeStruct((kv, out), f32),
        scratch_shapes=[pltpu.VMEM((out, kv), f32)],
        compiler_params=pltpu.CompilerParams(vmem_limit_bytes=VMEM_BYTES),
        name="weight_grad",
    )(grads_a, grads_a, grads_b, grads_b, featt)


def on_device(
    vlm_rows, images, action_hidden, lengths, vlm_weight, kv_weight, query_weight, context_grad
):
    _, slot_rows, width = vlm_rows.shape
    width_act = query_weight.shape[0]
    col = lax.axis_index("dp").astype(jnp.int32).reshape(1)

    weights = lax.all_gather(
        jnp.concatenate([vlm_weight.T, kv_weight.T], axis=1), "fsdp", axis=0, tiled=False
    )
    rows_a = gather_group(vlm_rows[0], MIRROR)
    rows_b = send(rows_a, CORE)
    normed_a, resid_a = normalize(rows_a, col)
    normed_b, resid_b = normalize(rows_b, col)
    queries = lax.dot_general(
        action_hidden[0], query_weight, (((1,), (1,)), ((), ())), preferred_element_type=f32
    ).astype(bf16)
    featt, part_a, part_b = layer(normed_a, normed_b, resid_a, resid_b, weights)

    featt_all = lax.all_gather(featt, "fsdp", axis=0, tiled=False)

    both = part_a + send(part_b, CORE).astype(f32)
    both = both.reshape(4, 2, slot_rows, 2 * width_act)
    mine = both[0]
    for e in (1, 2, 3):
        mine = mine + send(both[e].astype(bf16), ALONG_X[e]).astype(f32)
    other = send(mine[1].astype(bf16), MIRROR)

    context, grads = attention(mine[0], other, queries, images, lengths, context_grad[0])

    grads = lax.all_to_all(grads, "fsdp", 0, 0, tiled=True)
    grads_a = gather_group(grads, HALF)
    grads_b = send(grads_a, CORE)
    kv_weight_grad = weight_grad(grads_a, grads_b, featt_all)
    return (context[None], kv_weight_grad)


def solution(mesh):
    in_specs = (
        P(("dp", "fsdp"), None, None),
        P(("dp", "fsdp")),
        P(("dp", "fsdp"), None, None),
        P(("dp", "fsdp")),
        P("dp", "fsdp"),
        P("fsdp", "dp"),
        P(),
        P(("dp", "fsdp"), None, None),
    )
    out_specs = (P(("dp", "fsdp"), None, None), P("fsdp", "dp"))
    return jax.shard_map(
        on_device, mesh=mesh, in_specs=in_specs, out_specs=out_specs, check_vma=False
    )
```

```python
import jax
import jax.numpy as jnp
from jax import lax
from jax.experimental import pallas as pl
from jax.experimental.pallas import tpu as pltpu
from jax.sharding import PartitionSpec as P

HEAD_DIM = 48
IMG_TOK = 16
ACT = 16
AXES = ("dp", "fsdp")

eps = 1e-06
masked_value = -1e30
bf16 = jnp.bfloat16
f32 = jnp.float32
MIB = 1024 * 1024


def pairs(step):
    table = []
    for i in range(256):
        h, x, c, l, y = step(i >> 7, (i >> 5) & 3, (i >> 4) & 1, (i >> 2) & 3, i & 3)
        table.append((i, h << 7 | x << 5 | c << 4 | l << 2 | y))
    return table


CORE = pairs(lambda h, x, c, l, y: (h, x, c ^ 1, l, y))
MIRROR = pairs(lambda h, x, c, l, y: (h ^ 1, x, c, l ^ 3, y))
HALF = pairs(lambda h, x, c, l, y: (h ^ 1, x, c, l, y))
ALONG_X = [pairs(lambda h, x, c, l, y, e=e: (h, x ^ e, c, l, y)) for e in range(4)]
ALONG_Y = [pairs(lambda h, x, c, l, y, e=e: (h, x, c, l, y ^ e)) for e in range(4)]
ALONG_Z = [pairs(lambda h, x, c, l, y, e=e: (h, x, c, l ^ e, y)) for e in range(4)]


def send(array, table):
    return lax.ppermute(array, AXES, table)


def gather_along(own, tables):
    return jnp.stack([own] + [send(own, tables[e]) for e in (1, 2, 3)])


def params(mib):
    return pltpu.CompilerParams(vmem_limit_bytes=mib * MIB)


def norm_kernel(place_ref, rows_ref, normed_ref, resid_ref):
    widened = rows_ref[0].astype(f32)
    mean = jnp.mean(widened * widened, axis=-1, keepdims=True)
    normed = (widened * lax.rsqrt(mean + eps)).astype(bf16)
    blocks, _, depth = normed_ref.shape
    for f in range(blocks):
        normed_ref[f] = normed[:, f * depth : (f + 1) * depth]

        @pl.when(place_ref[0] == f)
        def _():
            resid_ref[...] = rows_ref[0, :, f * depth : (f + 1) * depth]


def normalize(rows, place):
    slots, height, width = rows.shape
    depth = width // 16
    return pl.pallas_call(
        norm_kernel,
        grid=(slots,),
        in_specs=[
            pl.BlockSpec(memory_space=pltpu.SMEM),
            pl.BlockSpec((1, height, width), lambda i: (i, 0, 0)),
        ],
        out_specs=[
            pl.BlockSpec((16, height, depth), lambda i: (0, i, 0)),
            pl.BlockSpec((height, depth), lambda i: (i, 0)),
        ],
        out_shape=[
            jax.ShapeDtypeStruct((16, slots * height, depth), bf16),
            jax.ShapeDtypeStruct((slots * height, depth), bf16),
        ],
        compiler_params=params(12),
        name="norm",
    )(place, rows)


def layer_kernel(*refs):
    normed_refs, resid_refs = refs[:4], refs[4:8]
    w_ref, feature_ref, featt_ref, kvw_ref, acc = refs[8:]
    step = pl.program_id(0)
    out = feature_ref.shape[1]
    total = None
    for k in range(w_ref.shape[0]):
        rows = jnp.concatenate([ref[k] for ref in normed_refs], axis=0)
        term = jnp.dot(rows, w_ref[k, :, :out], preferred_element_type=f32)
        total = term if total is None else total + term
    kvw_ref[0] = jnp.concatenate([w_ref[k, :, out:] for k in range(w_ref.shape[0])], axis=1)

    @pl.when(step == 0)
    def _():
        acc[...] = total

    @pl.when(step > 0)
    def _():
        acc[...] += total

    @pl.when(step == pl.num_programs(0) - 1)
    def _():
        pre = acc[...]
        resid = jnp.concatenate([ref[...] for ref in resid_refs], axis=0).astype(f32)
        feature = (resid + pre / (1.0 + jnp.exp(-pre))).astype(bf16)
        feature_ref[...] = feature
        featt_ref[...] = feature.T


def layer(normed, resid, weights):
    blocks, height, depth = normed[0].shape
    rows, out, wide, per = 4 * height, resid[0].shape[1], weights.shape[2], 4
    kv = (wide - out) * per

    def whole(shape):
        return pl.BlockSpec(shape, lambda k: (0, 0))

    return pl.pallas_call(
        layer_kernel,
        grid=(blocks // per,),
        in_specs=[pl.BlockSpec((per, height, depth), lambda k: (k, 0, 0))] * 4
        + [whole(resid[0].shape)] * 4
        + [pl.BlockSpec((per, depth, wide), lambda k: (k, 0, 0))],
        out_specs=[
            whole((rows, out)),
            whole((out, rows)),
            pl.BlockSpec((1, depth, kv), lambda k: (k, 0, 0)),
        ],
        out_shape=[
            jax.ShapeDtypeStruct((rows, out), bf16),
            jax.ShapeDtypeStruct((out, rows), bf16),
            jax.ShapeDtypeStruct((blocks // per, depth, kv), bf16),
        ],
        scratch_shapes=[pltpu.VMEM((rows, out), f32)],
        compiler_params=params(56),
        name="layer",
    )(*normed, *resid, weights)


def project_kernel(feature_ref, w_ref, out_ref):
    out_ref[...] = jnp.dot(feature_ref[...], w_ref[0], preferred_element_type=f32).astype(
        out_ref.dtype
    )


def project(feature, half, weights, dtype):
    rows, depth = feature.shape[0] // 2, feature.shape[1]
    blocks, _, kv = weights.shape
    return pl.pallas_call(
        project_kernel,
        grid=(blocks,),
        in_specs=[
            pl.BlockSpec((rows, depth), lambda i: (half, 0)),
            pl.BlockSpec((1, depth, kv), lambda i: (i, 0, 0)),
        ],
        out_specs=pl.BlockSpec((rows, kv), lambda i: (0, i)),
        out_shape=jax.ShapeDtypeStruct((rows, blocks * kv), dtype),
        compiler_params=params(16),
        name="project",
    )(feature, weights)


def attention_kernel(
    place_ref, images_ref, lengths_ref, own_ref, other_ref, q_ref, cg_ref, context_ref, grads_ref
):
    key_rows, width = own_ref.shape
    width_act = width // 2
    qrows = q_ref.shape[0]
    heads = 8
    cols = heads * HEAD_DIM
    scale = HEAD_DIM ** (-0.5)
    piece = width // 16
    y = place_ref[2]
    last = (((1,), (1,)), ((), ()))
    first = (((0,), (0,)), ((), ()))
    kv = (own_ref[...] + other_ref[...].astype(f32)).astype(bf16)
    row_head = lax.broadcasted_iota(jnp.int32, (heads * key_rows, cols), 0) // key_rows
    col_head = lax.broadcasted_iota(jnp.int32, (heads * key_rows, cols), 1) // HEAD_DIM
    same = row_head == col_head
    key_live = (
        lax.broadcasted_iota(jnp.int32, (heads, key_rows, qrows), 1) < images_ref[0] * IMG_TOK
    )
    query_live = lax.broadcasted_iota(jnp.int32, (qrows, cols), 0) % ACT < lengths_ref[0]

    def by_head(flat):
        return flat.reshape(heads, key_rows, qrows)

    def spread(rows):
        return jnp.where(same, jnp.concatenate([rows] * heads, axis=0), jnp.zeros((), bf16))

    def collapse(big):
        return jnp.sum(jnp.where(same, big, 0.0).reshape(heads, key_rows, cols), axis=0)

    for g in range(width_act // cols):
        at = slice(g * cols, (g + 1) * cols)
        keys = spread(kv[:, g * cols : (g + 1) * cols])
        values = spread(kv[:, width_act + g * cols : width_act + (g + 1) * cols])
        queries = q_ref[:, at]
        grad_in = jnp.where(query_live, cg_ref[:, at], jnp.zeros((), bf16))
        scores = by_head(lax.dot_general(keys, queries, last, preferred_element_type=f32) * scale)
        scores = jnp.where(key_live, scores, masked_value)
        exponent = jnp.exp(scores - jnp.max(scores, axis=1, keepdims=True))
        probs = exponent / jnp.sum(exponent, axis=1, keepdims=True)
        probs_low = probs.astype(bf16).reshape(heads * key_rows, qrows)
        mixed = lax.dot_general(probs_low, values, first, preferred_element_type=f32)
        context_ref[:, at] = jnp.where(query_live, mixed, 0.0).astype(bf16)
        prob_grad = by_head(lax.dot_general(values, grad_in, last, preferred_element_type=f32))
        centre = jnp.sum(prob_grad * probs, axis=1, keepdims=True)
        score_grad = (probs * (prob_grad - centre)).astype(bf16).reshape(heads * key_rows, qrows)
        value_grad = collapse(jnp.dot(probs_low, grad_in, preferred_element_type=f32)).astype(bf16)
        key_grad = jnp.dot(score_grad, queries, preferred_element_type=f32)
        key_grad = (collapse(key_grad) * scale).astype(bf16)
        per = cols // piece
        for start, grad in ((g * per, key_grad), (width_act // piece + g * per, value_grad)):
            for j in range(per):
                f = start + j
                column = f // 4 * piece
                grads_ref[(f % 4) ^ y, :, column : column + piece] = grad[
                    :, j * piece : (j + 1) * piece
                ]


def attention(own, other, queries, images, lengths, context_grad, place):
    key_rows, width = own.shape
    smem, vmem = pl.BlockSpec(memory_space=pltpu.SMEM), pl.BlockSpec(memory_space=pltpu.VMEM)
    return pl.pallas_call(
        attention_kernel,
        in_specs=[smem, smem, smem, vmem, vmem, vmem, vmem],
        out_specs=[vmem, vmem],
        out_shape=[
            jax.ShapeDtypeStruct(queries.shape, bf16),
            jax.ShapeDtypeStruct((4, key_rows, width // 4), bf16),
        ],
        compiler_params=params(24),
        name="attention",
    )(place, images, lengths, own, other, queries, context_grad)


def weight_grad_kernel(place_ref, a_ref, b_ref, featt_ref, own_ref, sends_ref, acc):
    step = pl.program_id(0)
    l, y = place_ref[1], place_ref[2]
    wide = acc.shape[1]
    packed = [ref[:, m, 0] for ref in (a_ref, b_ref) for m in range(2)]
    grads = jnp.concatenate(packed, axis=0).reshape(-1, wide)
    term = jnp.dot(featt_ref[0], grads, preferred_element_type=f32)

    @pl.when(step == 0)
    def _():
        acc[...] = term

    @pl.when(step > 0)
    def _():
        acc[...] += term

    @pl.when(step == pl.num_programs(0) - 1)
    def _():
        total = acc[...].T
        kv = wide // 4
        for fl in range(4):
            block = total[fl * kv : (fl + 1) * kv]
            sends_ref[fl ^ l] = block.astype(bf16)

            @pl.when(l == fl)
            def _():
                own_ref[...] = block


def weight_grad(grads_a, grads_b, featt, place):
    blocks, out, rows = featt.shape
    key_rows, wide = grads_a.shape[-2:]
    kv = wide // 4
    near = pl.BlockSpec((4, 2, 1, key_rows, wide), lambda i, place: (0, 0, i ^ place[2], 0, 0))
    return pl.pallas_call(
        weight_grad_kernel,
        grid_spec=pltpu.PrefetchScalarGridSpec(
            num_scalar_prefetch=1,
            grid=(blocks,),
            in_specs=[
                near,
                near,
                pl.BlockSpec((1, out, rows), lambda i, place: (i, 0, 0)),
            ],
            out_specs=[
                pl.BlockSpec((kv, out), lambda i, place: (0, 0)),
                pl.BlockSpec((4, kv, out), lambda i, place: (0, 0, 0)),
            ],
            scratch_shapes=[pltpu.VMEM((out, wide), f32)],
        ),
        out_shape=[
            jax.ShapeDtypeStruct((kv, out), f32),
            jax.ShapeDtypeStruct((4, kv, out), bf16),
        ],
        compiler_params=params(16),
        name="weight_grad",
    )(place, grads_a, grads_b, featt)


Y_GROUPS = [[l * 4 + y for y in range(4)] for l in range(4)]


def on_device(
    vlm_rows, images, action_hidden, lengths, vlm_weight, kv_weight, query_weight, context_grad
):
    _, slot_rows, width = vlm_rows.shape
    width_act = query_weight.shape[0]
    dp, fsdp = lax.axis_index("dp"), lax.axis_index("fsdp")
    place = jnp.stack([dp, fsdp // 4, fsdp % 4]).astype(jnp.int32)

    weights = lax.all_gather(
        jnp.concatenate([vlm_weight.T, kv_weight.T], axis=1), "fsdp", axis=0, tiled=False
    )
    mirrored = send(vlm_rows[0], MIRROR)
    own_a = gather_along(vlm_rows[0], ALONG_X)
    mirrored, own_a = lax.optimization_barrier((mirrored, own_a))
    far_a = gather_along(mirrored, ALONG_X)
    own_b = send(own_a, CORE)
    normed, resid = zip(normalize(own_a, place), normalize(own_b, place))
    far_a, normed, resid = lax.optimization_barrier((far_a, normed, resid))
    far_b = send(far_a, CORE)
    more, rest = zip(normalize(far_a, place), normalize(far_b, place))
    normed = (normed[0], more[0], normed[1], more[1])
    resid = (resid[0], rest[0], resid[1], rest[1])
    queries = lax.dot_general(
        action_hidden[0], query_weight, (((1,), (1,)), ((), ())), preferred_element_type=f32
    ).astype(bf16)
    queries, normed = lax.optimization_barrier((queries, normed))
    feature, featt, kv_weights = layer(normed, resid, weights)
    featt_all = lax.all_gather(
        featt, "fsdp", axis=0, tiled=False, axis_index_groups=Y_GROUPS
    )

    part_b = project(feature, 1, kv_weights, bf16)
    swapped = send(part_b, CORE)
    part_a = project(feature, 0, kv_weights, f32)
    both = (part_a + swapped.astype(f32)).reshape(2, 4, slot_rows, 2 * width_act)
    mine = both[:, 0]
    for e in (1, 2, 3):
        mine = mine + send(both[:, e].astype(bf16), ALONG_X[e]).astype(f32)
    other = send(mine[1].astype(bf16), MIRROR)

    context, grads = attention(
        mine[0], other, queries, images, lengths, context_grad[0], place
    )

    by_y = jnp.stack([grads[0]] + [send(grads[e], ALONG_Y[e]) for e in (1, 2, 3)])
    grads_a = gather_along(jnp.stack([by_y, send(by_y, MIRROR)]), ALONG_X)
    grads_b = send(grads_a, CORE)
    kv_weight_grad, sums = weight_grad(grads_a, grads_b, featt_all, place)
    for e in (1, 2, 3):
        kv_weight_grad = kv_weight_grad + send(sums[e], ALONG_Z[e]).astype(f32)
    return (context[None], kv_weight_grad)


def solution(mesh):
    in_specs = (
        P(("dp", "fsdp"), None, None),
        P(("dp", "fsdp")),
        P(("dp", "fsdp"), None, None),
        P(("dp", "fsdp")),
        P("dp", "fsdp"),
        P("fsdp", "dp"),
        P(),
        P(("dp", "fsdp"), None, None),
    )
    out_specs = (P(("dp", "fsdp"), None, None), P("fsdp", "dp"))
    return jax.shard_map(
        on_device, mesh=mesh, in_specs=in_specs, out_specs=out_specs, check_vma=False
    )
```

```python
import functools

import jax
import jax.numpy as jnp
from jax import lax
from jax.experimental import pallas as pl
from jax.experimental.pallas import tpu as pltpu
from jax.sharding import PartitionSpec as P

HEAD_DIM = 48
IMG_TOK = 16
ACT = 16
AXES = ("dp", "fsdp")

eps = 1e-06
masked_value = -1e30
bf16 = jnp.bfloat16
f32 = jnp.float32
MIB = 1024 * 1024


def pairs(step):
    table = []
    for i in range(256):
        h, x, c, l, y = step(i >> 7, (i >> 5) & 3, (i >> 4) & 1, (i >> 2) & 3, i & 3)
        table.append((i, h << 7 | x << 5 | c << 4 | l << 2 | y))
    return table


CORE = pairs(lambda h, x, c, l, y: (h, x, c ^ 1, l, y))
MIRROR = pairs(lambda h, x, c, l, y: (h ^ 1, x, c, l ^ 3, y))
HALF = pairs(lambda h, x, c, l, y: (h ^ 1, x, c, l, y))
ALONG_X = [pairs(lambda h, x, c, l, y, e=e: (h, x ^ e, c, l, y)) for e in range(4)]
ALONG_Y = [pairs(lambda h, x, c, l, y, e=e: (h, x, c, l, y ^ e)) for e in range(4)]
ALONG_Z = [pairs(lambda h, x, c, l, y, e=e: (h, x, c, l ^ e, y)) for e in range(4)]


def send(array, table):
    return lax.ppermute(array, AXES, table)


def gather_along(own, tables):
    return jnp.stack([own] + [send(own, tables[e]) for e in (1, 2, 3)])


def params(mib):
    return pltpu.CompilerParams(vmem_limit_bytes=mib * MIB)


def norm_kernel(place_ref, rows_ref, normed_ref, resid_ref):
    widened = rows_ref[...].astype(f32)
    mean = jnp.mean(widened * widened, axis=-1, keepdims=True)
    normed_ref[...] = (widened * lax.rsqrt(mean + eps)).astype(bf16)
    depth = resid_ref.shape[1]
    for f in range(rows_ref.shape[1] // depth):

        @pl.when(place_ref[0] == f)
        def _():
            resid_ref[...] = rows_ref[:, f * depth : (f + 1) * depth]


def normalize(rows, place):
    height, width = rows.shape
    depth, per = width // 16, 64
    return pl.pallas_call(
        norm_kernel,
        grid=(height // per,),
        in_specs=[
            pl.BlockSpec(memory_space=pltpu.SMEM),
            pl.BlockSpec((per, width), lambda i: (i, 0)),
        ],
        out_specs=[
            pl.BlockSpec((per, width), lambda i: (i, 0)),
            pl.BlockSpec((per, depth), lambda i: (i, 0)),
        ],
        out_shape=[
            jax.ShapeDtypeStruct((height, width), bf16),
            jax.ShapeDtypeStruct((height, depth), bf16),
        ],
        compiler_params=params(56),
        name="norm",
    )(place, rows)


def layer_kernel(place_ref, *refs, finish):
    normed_refs, piece_refs = refs[:2], refs[2:10]
    resid_refs, acc_ref = refs[10:12], refs[12]
    kvw_ref, *out_refs, weights = refs[13:]
    y = place_ref[2]
    out = acc_ref.shape[1]
    half = piece_refs[0].shape[0]
    depth = 2 * half
    for i, ref in enumerate(piece_refs):
        at = pl.multiple_of((y ^ (i // 2)) * depth + i % 2 * half, 32)
        weights[pl.ds(at, half)] = ref[...]
    kvw_ref[...] = jnp.concatenate(
        [weights[f * depth : (f + 1) * depth, out:] for f in range(4)], axis=1
    )
    rows = normed_refs[0].shape[0]
    for i, (normed_ref, resid_ref) in enumerate(zip(normed_refs, resid_refs)):
        at = slice(i * rows, (i + 1) * rows)
        total = acc_ref[at] + jnp.dot(
            normed_ref[...], weights[:, :out], preferred_element_type=f32
        )
        if finish:
            feature_ref, featt_ref = out_refs
            silu = total / (1.0 + jnp.exp(-total))
            feature = (resid_ref[...].astype(f32) + silu).astype(bf16)
            feature_ref[at] = feature
            featt_ref[:, at] = feature.T
        else:
            out_refs[0][at] = total


def layer(place, normed, pieces, resid, acc, e, finish):
    rows, out = acc.shape
    wide = pieces[0][0].shape[1]
    kv = wide - out
    depth = normed[0].shape[1] // 16
    half = depth // 2

    def whole(shape):
        return pl.BlockSpec(shape, lambda i, place: (0, 0))

    if finish:
        shapes = [((rows, out), bf16), ((out, rows), bf16)]
    else:
        shapes = [((rows, out), f32)]
    shapes = [((depth, 4 * kv), bf16)] + shapes
    return pl.pallas_call(
        functools.partial(layer_kernel, finish=finish),
        grid_spec=pltpu.PrefetchScalarGridSpec(
            num_scalar_prefetch=1,
            grid=(1,),
            in_specs=[
                pl.BlockSpec((rows // 2, 4 * depth), lambda i, place: (0, place[1] ^ e)),
            ]
            * 2
            + [
                pl.BlockSpec((half, wide), lambda i, place, at=at: (at, 0)) for _, at in pieces
            ]
            + [whole(r.shape) for r in resid]
            + [whole(acc.shape)],
            out_specs=[whole(shape) for shape, _ in shapes],
            scratch_shapes=[pltpu.VMEM((4 * depth, wide), bf16)],
        ),
        out_shape=[jax.ShapeDtypeStruct(shape, dtype) for shape, dtype in shapes],
        compiler_params=params(32),
        name="layer",
    )(place, *normed, *[array for array, _ in pieces], *resid, acc)


def project_kernel(feature_ref, *refs):
    out_ref = refs[-1]
    kv = refs[0].shape[1]
    for e, w_ref in enumerate(refs[:-1]):
        out_ref[:, e * kv : (e + 1) * kv] = jnp.dot(
            feature_ref[...], w_ref[...], preferred_element_type=f32
        ).astype(out_ref.dtype)


def project(feature, half, weights, dtype):
    rows, depth = feature.shape[0] // 2, feature.shape[1]
    kv = weights[0].shape[1]
    return pl.pallas_call(
        project_kernel,
        grid=(1,),
        in_specs=[pl.BlockSpec((rows, depth), lambda i: (half, 0))]
        + [pl.BlockSpec((depth, kv), lambda i: (0, 0))] * 4,
        out_specs=pl.BlockSpec((rows, 4 * kv), lambda i: (0, 0)),
        out_shape=jax.ShapeDtypeStruct((rows, 4 * kv), dtype),
        compiler_params=params(20),
        name="project",
    )(feature, *weights)


def attention_kernel(
    place_ref, images_ref, lengths_ref, own_ref, other_ref, q_ref, cg_ref, context_ref, grads_ref, kvs
):
    key_rows, width = own_ref.shape
    width_act = width // 2
    qrows = q_ref.shape[0]
    heads = 8
    cols = heads * HEAD_DIM
    scale = HEAD_DIM ** (-0.5)
    piece = width // 16
    l, y = place_ref[1], place_ref[2]
    last = (((1,), (1,)), ((), ()))
    first = (((0,), (0,)), ((), ()))
    wide = width // 4
    for e in range(4):
        own = own_ref[:, e * wide : (e + 1) * wide]
        other = other_ref[:, (3 - e) * wide : (4 - e) * wide].astype(f32)
        kvs[e] = (own + other).astype(bf16)
    row_head = lax.broadcasted_iota(jnp.int32, (heads * key_rows, cols), 0) // key_rows
    col_head = lax.broadcasted_iota(jnp.int32, (heads * key_rows, cols), 1) // HEAD_DIM
    same = row_head == col_head
    key_live = (
        lax.broadcasted_iota(jnp.int32, (heads, key_rows, qrows), 1) < images_ref[0] * IMG_TOK
    )
    query_live = lax.broadcasted_iota(jnp.int32, (qrows, cols), 0) % ACT < lengths_ref[0]

    def by_head(flat):
        return flat.reshape(heads, key_rows, qrows)

    def spread(rows):
        return jnp.where(same, jnp.concatenate([rows] * heads, axis=0), jnp.zeros((), bf16))

    def collapse(big):
        return jnp.sum(jnp.where(same, big, 0.0).reshape(heads, key_rows, cols), axis=0)

    for g in range(width_act // cols):
        at = slice(g * cols, (g + 1) * cols)
        column = slice(g % 2 * cols, (g % 2 + 1) * cols)
        keys = spread(kvs[(g // 2) ^ l, :, column])
        values = spread(kvs[(2 + g // 2) ^ l, :, column])
        queries = q_ref[:, at]
        grad_in = jnp.where(query_live, cg_ref[:, at], jnp.zeros((), bf16))
        scores = by_head(lax.dot_general(keys, queries, last, preferred_element_type=f32) * scale)
        scores = jnp.where(key_live, scores, masked_value)
        exponent = jnp.exp(scores - jnp.max(scores, axis=1, keepdims=True))
        probs = exponent / jnp.sum(exponent, axis=1, keepdims=True)
        probs_low = probs.astype(bf16).reshape(heads * key_rows, qrows)
        mixed = lax.dot_general(probs_low, values, first, preferred_element_type=f32)
        context_ref[:, at] = jnp.where(query_live, mixed, 0.0).astype(bf16)
        prob_grad = by_head(lax.dot_general(values, grad_in, last, preferred_element_type=f32))
        centre = jnp.sum(prob_grad * probs, axis=1, keepdims=True)
        score_grad = (probs * (prob_grad - centre)).astype(bf16).reshape(heads * key_rows, qrows)
        value_grad = collapse(jnp.dot(probs_low, grad_in, preferred_element_type=f32)).astype(bf16)
        key_grad = jnp.dot(score_grad, queries, preferred_element_type=f32)
        key_grad = (collapse(key_grad) * scale).astype(bf16)
        per = cols // piece
        for start, grad in ((g * per, key_grad), (width_act // piece + g * per, value_grad)):
            for j in range(per):
                f = start + j
                column = f // 4 * piece
                grads_ref[(f % 4) ^ y, :, column : column + piece] = grad[
                    :, j * piece : (j + 1) * piece
                ]


def attention(own, other, queries, images, lengths, context_grad, place):
    key_rows, width = own.shape
    smem, vmem = pl.BlockSpec(memory_space=pltpu.SMEM), pl.BlockSpec(memory_space=pltpu.VMEM)
    return pl.pallas_call(
        attention_kernel,
        in_specs=[smem, smem, smem, vmem, vmem, vmem, vmem],
        out_specs=[vmem, vmem],
        out_shape=[
            jax.ShapeDtypeStruct(queries.shape, bf16),
            jax.ShapeDtypeStruct((4, key_rows, width // 4), bf16),
        ],
        scratch_shapes=[pltpu.VMEM((4, key_rows, width // 4), bf16)],
        compiler_params=params(24),
        name="attention",
    )(place, images, lengths, own, other, queries, context_grad)


def weight_grad_kernel(place_ref, a_ref, b_ref, featt_ref, own_ref, sends_ref, acc):
    step = pl.program_id(0)
    l, y = place_ref[1], place_ref[2]
    wide = acc.shape[1]
    grads = jnp.concatenate([ref[:, :, 0].reshape(-1, wide) for ref in (a_ref, b_ref)], axis=0)
    term = jnp.dot(featt_ref[0], grads, preferred_element_type=f32)

    @pl.when(step == 0)
    def _():
        acc[...] = term

    @pl.when(step > 0)
    def _():
        acc[...] += term

    @pl.when(step == pl.num_programs(0) - 1)
    def _():
        total = acc[...].T
        kv = wide // 4
        for fl in range(4):
            block = total[fl * kv : (fl + 1) * kv]
            sends_ref[fl ^ l] = block.astype(bf16)

            @pl.when(l == fl)
            def _():
                own_ref[...] = block


def weight_grad(grads_a, grads_b, featt, place):
    blocks, out, rows = featt.shape
    key_rows, wide = grads_a.shape[-2:]
    kv = wide // 4
    near = pl.BlockSpec((4, 2, 1, key_rows, wide), lambda i, place: (0, 0, i, 0, 0))
    return pl.pallas_call(
        weight_grad_kernel,
        grid_spec=pltpu.PrefetchScalarGridSpec(
            num_scalar_prefetch=1,
            grid=(blocks,),
            in_specs=[
                near,
                near,
                pl.BlockSpec((1, out, rows), lambda i, place: (i, 0, 0)),
            ],
            out_specs=[
                pl.BlockSpec((kv, out), lambda i, place: (0, 0)),
                pl.BlockSpec((4, kv, out), lambda i, place: (0, 0, 0)),
            ],
            scratch_shapes=[pltpu.VMEM((out, wide), f32)],
        ),
        out_shape=[
            jax.ShapeDtypeStruct((kv, out), f32),
            jax.ShapeDtypeStruct((4, kv, out), bf16),
        ],
        compiler_params=params(16),
        name="weight_grad",
    )(place, grads_a, grads_b, featt)


def on_device(
    vlm_rows, images, action_hidden, lengths, vlm_weight, kv_weight, query_weight, context_grad
):
    _, slot_rows, width = vlm_rows.shape
    width_act = query_weight.shape[0]
    dp, fsdp = lax.axis_index("dp"), lax.axis_index("fsdp")
    place = jnp.stack([dp, fsdp // 4, fsdp % 4]).astype(jnp.int32)

    block = jnp.concatenate([vlm_weight.T, kv_weight.T], axis=1)
    half = block.shape[0] // 2

    def around(before, w):
        up, down = before
        low, high = down[-2 * half : -half], up[-half:]
        if w is not None:
            low, high = jnp.concatenate([low, w]), jnp.concatenate([high, w])
        return send(low, ALONG_Y[1]), send(high, ALONG_Y[3])

    rows = vlm_rows[0]
    y0 = send(block, ALONG_Y[1]), send(block, ALONG_Y[3])
    z1, mirrored = send(block, ALONG_Z[1]), send(rows, MIRROR)
    y0, z1, mirrored, block = lax.optimization_barrier((y0, z1, mirrored, block))

    rows = jnp.stack([rows, mirrored])
    y1, z2 = around(y0, z1), send(block, ALONG_Z[2])
    x1, x3 = send(rows, ALONG_X[1]), send(rows, ALONG_X[3])
    y1, z2, x1, x3, block, rows = lax.optimization_barrier((y1, z2, x1, x3, block, rows))

    y2, z3 = around(y1, z2), send(block, ALONG_Z[3])
    x2 = send(rows, ALONG_X[2])
    queries = lax.dot_general(
        action_hidden[0], query_weight, (((1,), (1,)), ((), ())), preferred_element_type=f32
    ).astype(bf16)
    y2, z3, x2, queries = lax.optimization_barrier((y2, z3, x2, queries))

    y3 = around(y2, z3)
    rows_a = jnp.stack([rows, x1, x2, x3]).reshape(-1, width)
    rows_b = send(rows_a, CORE)
    normed, resid = zip(normalize(rows_a, place), normalize(rows_b, place))
    acc = jnp.zeros((16 * slot_rows, vlm_weight.shape[0]), f32)
    kv_weights = []

    def add(e, own, near, after, acc):
        first = near[0].shape[0] // half - 2
        pieces = [(own, 0), (own, 1), (near[0], first), (near[0], first + 1)]
        pieces += [(after[0], 0), (after[1], 0), (near[1], first), (near[1], first + 1)]
        kvw, *rest = layer(place, normed, pieces, resid, acc, e, e == 3)
        kv_weights.append(kvw)
        return rest

    (acc,) = add(0, block, y0, y1, acc)
    (acc,) = add(1, z1, y1, y2, acc)
    y3, acc = lax.optimization_barrier((y3, acc))

    y4 = around(y3, None)
    (acc,) = add(2, z2, y2, y3, acc)
    feature, featt = add(3, z3, y3, y4, acc)

    part_b = project(feature, 1, kv_weights, bf16)
    swapped = send(part_b, CORE)
    part_a = project(feature, 0, kv_weights, f32)
    both = (part_a + swapped.astype(f32)).reshape(4, 2, slot_rows, 2 * width_act)
    both, featt = lax.optimization_barrier((both, featt))
    sums = [send(both[e].astype(bf16), ALONG_X[e]) for e in (1, 2, 3)]
    featt_all = gather_along(featt, ALONG_Y)
    sums, featt_all = lax.optimization_barrier((sums, featt_all))
    mine = both[0]
    for term in sums:
        mine = mine + term.astype(f32)
    other = send(mine[1].astype(bf16), MIRROR)

    context, grads = attention(
        mine[0], other, queries, images, lengths, context_grad[0], place
    )

    by_y = jnp.stack([grads[0]] + [send(grads[e], ALONG_Y[e]) for e in (1, 2, 3)])
    grads_a = gather_along(jnp.stack([by_y, send(by_y, MIRROR)]), ALONG_X)
    grads_b = send(grads_a, CORE)
    kv_weight_grad, sums = weight_grad(grads_a, grads_b, featt_all, place)
    for e in (1, 2, 3):
        kv_weight_grad = kv_weight_grad + send(sums[e], ALONG_Z[e]).astype(f32)
    return (context[None], kv_weight_grad)


def solution(mesh):
    in_specs = (
        P(("dp", "fsdp"), None, None),
        P(("dp", "fsdp")),
        P(("dp", "fsdp"), None, None),
        P(("dp", "fsdp")),
        P("dp", "fsdp"),
        P("fsdp", "dp"),
        P(),
        P(("dp", "fsdp"), None, None),
    )
    out_specs = (P(("dp", "fsdp"), None, None), P("fsdp", "dp"))
    return jax.shard_map(
        on_device, mesh=mesh, in_specs=in_specs, out_specs=out_specs, check_vma=False
    )
```

```python
import functools

import jax
import jax.numpy as jnp
from jax import lax
from jax.experimental import pallas as pl
from jax.experimental.pallas import tpu as pltpu
from jax.sharding import PartitionSpec as P

HEAD_DIM = 48
IMG_TOK = 16
ACT = 16
AXES = ("dp", "fsdp")

eps = 1e-06
masked_value = -1e30
bf16 = jnp.bfloat16
f32 = jnp.float32
MIB = 1024 * 1024


def pairs(step):
    table = []
    for i in range(256):
        h, x, c, l, y = step(i >> 7, (i >> 5) & 3, (i >> 4) & 1, (i >> 2) & 3, i & 3)
        table.append((i, h << 7 | x << 5 | c << 4 | l << 2 | y))
    return table


CORE = pairs(lambda h, x, c, l, y: (h, x, c ^ 1, l, y))
MIRROR = pairs(lambda h, x, c, l, y: (h ^ 1, x, c, l ^ 3, y))
HALF = pairs(lambda h, x, c, l, y: (h ^ 1, x, c, l, y))
ALONG_X = [pairs(lambda h, x, c, l, y, e=e: (h, x ^ e, c, l, y)) for e in range(4)]
ALONG_Y = [pairs(lambda h, x, c, l, y, e=e: (h, x, c, l, y ^ e)) for e in range(4)]
ALONG_Z = [pairs(lambda h, x, c, l, y, e=e: (h, x, c, l ^ e, y)) for e in range(4)]


def send(array, table):
    return lax.ppermute(array, AXES, table)


def gather_along(own, tables):
    return jnp.stack([own] + [send(own, tables[e]) for e in (1, 2, 3)])


def params(mib):
    return pltpu.CompilerParams(vmem_limit_bytes=mib * MIB)


def norm_kernel(place_ref, rows_ref, normed_ref, resid_ref):
    widened = rows_ref[...].astype(f32)
    mean = jnp.mean(widened * widened, axis=-1, keepdims=True)
    normed_ref[...] = (widened * lax.rsqrt(mean + eps)).astype(bf16)
    depth = resid_ref.shape[1]
    for f in range(rows_ref.shape[1] // depth):

        @pl.when(place_ref[0] == f)
        def _():
            resid_ref[...] = rows_ref[:, f * depth : (f + 1) * depth]


def normalize(rows, place):
    height, width = rows.shape
    depth, per = width // 16, 64
    return pl.pallas_call(
        norm_kernel,
        grid=(height // per,),
        in_specs=[
            pl.BlockSpec(memory_space=pltpu.SMEM),
            pl.BlockSpec((per, width), lambda i: (i, 0)),
        ],
        out_specs=[
            pl.BlockSpec((per, width), lambda i: (i, 0)),
            pl.BlockSpec((per, depth), lambda i: (i, 0)),
        ],
        out_shape=[
            jax.ShapeDtypeStruct((height, width), bf16),
            jax.ShapeDtypeStruct((height, depth), bf16),
        ],
        compiler_params=params(12),
        name="norm",
    )(place, rows)


def layer_kernel(place_ref, *refs, finish):
    normed_refs, piece_refs = refs[:4], refs[4:12]
    resid_refs, acc_ref = refs[12:16], refs[16]
    kvw_ref, *out_refs, weights = refs[17:]
    y = place_ref[2]
    out = acc_ref.shape[1]
    half = piece_refs[0].shape[0]
    depth = 2 * half
    for i, ref in enumerate(piece_refs):
        at = pl.multiple_of((y ^ (i // 2)) * depth + i % 2 * half, 32)
        weights[pl.ds(at, half)] = ref[...]
    kvw_ref[...] = jnp.concatenate(
        [weights[f * depth : (f + 1) * depth, out:] for f in range(4)], axis=1
    )
    normed = jnp.concatenate([ref[...] for ref in normed_refs], axis=0)
    total = acc_ref[...] + jnp.dot(normed, weights[:, :out], preferred_element_type=f32)
    if finish:
        feature_ref, featt_ref = out_refs
        resid = jnp.concatenate([ref[...] for ref in resid_refs], axis=0).astype(f32)
        feature = (resid + total / (1.0 + jnp.exp(-total))).astype(bf16)
        feature_ref[...] = feature
        featt_ref[...] = feature.T
    else:
        out_refs[0][...] = total


def layer(place, normed, pieces, resid, acc, e, finish):
    rows, out = acc.shape
    wide = pieces[0][0].shape[1]
    kv = wide - out
    depth = normed[0].shape[1] // 16
    half = depth // 2

    def whole(shape):
        return pl.BlockSpec(shape, lambda i, place: (0, 0))

    if finish:
        shapes = [((rows, out), bf16), ((out, rows), bf16)]
    else:
        shapes = [((rows, out), f32)]
    shapes = [((depth, 4 * kv), bf16)] + shapes
    return pl.pallas_call(
        functools.partial(layer_kernel, finish=finish),
        grid_spec=pltpu.PrefetchScalarGridSpec(
            num_scalar_prefetch=1,
            grid=(1,),
            in_specs=[
                pl.BlockSpec((rows // 4, 4 * depth), lambda i, place: (0, place[1] ^ e)),
            ]
            * 4
            + [
                pl.BlockSpec((half, wide), lambda i, place, at=at: (at, 0)) for _, at in pieces
            ]
            + [whole(r.shape) for r in resid]
            + [whole(acc.shape)],
            out_specs=[whole(shape) for shape, _ in shapes],
            scratch_shapes=[pltpu.VMEM((4 * depth, wide), bf16)],
        ),
        out_shape=[jax.ShapeDtypeStruct(shape, dtype) for shape, dtype in shapes],
        compiler_params=params(24),
        name="layer",
    )(place, *normed, *[array for array, _ in pieces], *resid, acc)


def project_kernel(feature_ref, *refs):
    out_ref = refs[-1]
    kv = refs[0].shape[1]
    for e, w_ref in enumerate(refs[:-1]):
        out_ref[:, e * kv : (e + 1) * kv] = jnp.dot(
            feature_ref[...], w_ref[...], preferred_element_type=f32
        ).astype(out_ref.dtype)


def project(feature, half, weights, dtype):
    rows, depth = feature.shape[0] // 2, feature.shape[1]
    kv = weights[0].shape[1]
    return pl.pallas_call(
        project_kernel,
        grid=(1,),
        in_specs=[pl.BlockSpec((rows, depth), lambda i: (half, 0))]
        + [pl.BlockSpec((depth, kv), lambda i: (0, 0))] * 4,
        out_specs=pl.BlockSpec((rows, 4 * kv), lambda i: (0, 0)),
        out_shape=jax.ShapeDtypeStruct((rows, 4 * kv), dtype),
        compiler_params=params(16),
        name="project",
    )(feature, *weights)


def attention_kernel(
    place_ref, images_ref, lengths_ref, own_ref, other_ref, q_ref, cg_ref, context_ref, grads_ref, kvs
):
    key_rows, width = own_ref.shape
    width_act = width // 2
    qrows = q_ref.shape[0]
    heads = 8
    cols = heads * HEAD_DIM
    scale = HEAD_DIM ** (-0.5)
    piece = width // 16
    l, y = place_ref[1], place_ref[2]
    last = (((1,), (1,)), ((), ()))
    first = (((0,), (0,)), ((), ()))
    wide = width // 4
    for e in range(4):
        own = own_ref[:, e * wide : (e + 1) * wide]
        other = other_ref[:, (3 - e) * wide : (4 - e) * wide].astype(f32)
        kvs[e] = (own + other).astype(bf16)
    row_head = lax.broadcasted_iota(jnp.int32, (heads * key_rows, cols), 0) // key_rows
    col_head = lax.broadcasted_iota(jnp.int32, (heads * key_rows, cols), 1) // HEAD_DIM
    same = row_head == col_head
    key_live = (
        lax.broadcasted_iota(jnp.int32, (heads, key_rows, qrows), 1) < images_ref[0] * IMG_TOK
    )
    query_live = lax.broadcasted_iota(jnp.int32, (qrows, cols), 0) % ACT < lengths_ref[0]

    def by_head(flat):
        return flat.reshape(heads, key_rows, qrows)

    def spread(rows):
        return jnp.where(same, jnp.concatenate([rows] * heads, axis=0), jnp.zeros((), bf16))

    def collapse(big):
        return jnp.sum(jnp.where(same, big, 0.0).reshape(heads, key_rows, cols), axis=0)

    for g in range(width_act // cols):
        at = slice(g * cols, (g + 1) * cols)
        column = slice(g % 2 * cols, (g % 2 + 1) * cols)
        keys = spread(kvs[(g // 2) ^ l, :, column])
        values = spread(kvs[(2 + g // 2) ^ l, :, column])
        queries = q_ref[:, at]
        grad_in = jnp.where(query_live, cg_ref[:, at], jnp.zeros((), bf16))
        scores = by_head(lax.dot_general(keys, queries, last, preferred_element_type=f32) * scale)
        scores = jnp.where(key_live, scores, masked_value)
        exponent = jnp.exp(scores - jnp.max(scores, axis=1, keepdims=True))
        probs = exponent / jnp.sum(exponent, axis=1, keepdims=True)
        probs_low = probs.astype(bf16).reshape(heads * key_rows, qrows)
        mixed = lax.dot_general(probs_low, values, first, preferred_element_type=f32)
        context_ref[:, at] = jnp.where(query_live, mixed, 0.0).astype(bf16)
        prob_grad = by_head(lax.dot_general(values, grad_in, last, preferred_element_type=f32))
        centre = jnp.sum(prob_grad * probs, axis=1, keepdims=True)
        score_grad = (probs * (prob_grad - centre)).astype(bf16).reshape(heads * key_rows, qrows)
        value_grad = collapse(jnp.dot(probs_low, grad_in, preferred_element_type=f32)).astype(bf16)
        key_grad = jnp.dot(score_grad, queries, preferred_element_type=f32)
        key_grad = (collapse(key_grad) * scale).astype(bf16)
        per = cols // piece
        for start, grad in ((g * per, key_grad), (width_act // piece + g * per, value_grad)):
            for j in range(per):
                f = start + j
                column = f // 4 * piece
                grads_ref[(f % 4) ^ y, :, column : column + piece] = grad[
                    :, j * piece : (j + 1) * piece
                ]


def attention(own, other, queries, images, lengths, context_grad, place):
    key_rows, width = own.shape
    smem, vmem = pl.BlockSpec(memory_space=pltpu.SMEM), pl.BlockSpec(memory_space=pltpu.VMEM)
    return pl.pallas_call(
        attention_kernel,
        in_specs=[smem, smem, smem, vmem, vmem, vmem, vmem],
        out_specs=[vmem, vmem],
        out_shape=[
            jax.ShapeDtypeStruct(queries.shape, bf16),
            jax.ShapeDtypeStruct((4, key_rows, width // 4), bf16),
        ],
        scratch_shapes=[pltpu.VMEM((4, key_rows, width // 4), bf16)],
        compiler_params=params(24),
        name="attention",
    )(place, images, lengths, own, other, queries, context_grad)


def weight_grad_kernel(place_ref, a_ref, b_ref, featt_ref, own_ref, sends_ref, acc):
    step = pl.program_id(0)
    l, y = place_ref[1], place_ref[2]
    wide = acc.shape[1]
    packed = [ref[:, m, 0] for ref in (a_ref, b_ref) for m in range(2)]
    grads = jnp.concatenate(packed, axis=0).reshape(-1, wide)
    term = jnp.dot(featt_ref[0], grads, preferred_element_type=f32)

    @pl.when(step == 0)
    def _():
        acc[...] = term

    @pl.when(step > 0)
    def _():
        acc[...] += term

    @pl.when(step == pl.num_programs(0) - 1)
    def _():
        total = acc[...].T
        kv = wide // 4
        for fl in range(4):
            block = total[fl * kv : (fl + 1) * kv]
            sends_ref[fl ^ l] = block.astype(bf16)

            @pl.when(l == fl)
            def _():
                own_ref[...] = block


def weight_grad(grads_a, grads_b, featt, place):
    blocks, out, rows = featt.shape
    key_rows, wide = grads_a.shape[-2:]
    kv = wide // 4
    near = pl.BlockSpec((4, 2, 1, key_rows, wide), lambda i, place: (0, 0, i, 0, 0))
    return pl.pallas_call(
        weight_grad_kernel,
        grid_spec=pltpu.PrefetchScalarGridSpec(
            num_scalar_prefetch=1,
            grid=(blocks,),
            in_specs=[
                near,
                near,
                pl.BlockSpec((1, out, rows), lambda i, place: (i, 0, 0)),
            ],
            out_specs=[
                pl.BlockSpec((kv, out), lambda i, place: (0, 0)),
                pl.BlockSpec((4, kv, out), lambda i, place: (0, 0, 0)),
            ],
            scratch_shapes=[pltpu.VMEM((out, wide), f32)],
        ),
        out_shape=[
            jax.ShapeDtypeStruct((kv, out), f32),
            jax.ShapeDtypeStruct((4, kv, out), bf16),
        ],
        compiler_params=params(16),
        name="weight_grad",
    )(place, grads_a, grads_b, featt)


def on_device(
    vlm_rows, images, action_hidden, lengths, vlm_weight, kv_weight, query_weight, context_grad
):
    _, slot_rows, width = vlm_rows.shape
    width_act = query_weight.shape[0]
    dp, fsdp = lax.axis_index("dp"), lax.axis_index("fsdp")
    place = jnp.stack([dp, fsdp // 4, fsdp % 4]).astype(jnp.int32)

    block = jnp.concatenate([vlm_weight.T, kv_weight.T], axis=1)
    half = block.shape[0] // 2

    def around(before, w):
        up, down = before
        low, high = down[-2 * half : -half], up[-half:]
        if w is not None:
            low, high = jnp.concatenate([low, w]), jnp.concatenate([high, w])
        return send(low, ALONG_Y[1]), send(high, ALONG_Y[3])

    def along_x(rows, e):
        return send(rows, ALONG_X[e])

    rows = vlm_rows[0]
    y0 = send(block, ALONG_Y[1]), send(block, ALONG_Y[3])
    z1, own1, own3 = send(block, ALONG_Z[1]), along_x(rows, 1), along_x(rows, 3)
    y0, z1, own1, own3, block, rows = lax.optimization_barrier(
        (y0, z1, own1, own3, block, rows)
    )

    y1, z2 = around(y0, z1), send(block, ALONG_Z[2])
    mirrored, own2 = send(rows, MIRROR), along_x(rows, 2)
    y1, z2, mirrored, own2, block = lax.optimization_barrier((y1, z2, mirrored, own2, block))

    y2, z3 = around(y1, z2), send(block, ALONG_Z[3])
    far1, far3 = along_x(mirrored, 1), along_x(mirrored, 3)
    own_a = jnp.concatenate([rows, own1, own2, own3])
    queries = lax.dot_general(
        action_hidden[0], query_weight, (((1,), (1,)), ((), ())), preferred_element_type=f32
    ).astype(bf16)
    own_a_normed = normalize(own_a, place)
    y2, z3, far1, far3, mirrored, queries, own_a, own_a_normed = lax.optimization_barrier(
        (y2, z3, far1, far3, mirrored, queries, own_a, own_a_normed)
    )

    y3, far2 = around(y2, z3), along_x(mirrored, 2)
    own_b = send(own_a, CORE)
    own_b_normed = normalize(own_b, place)
    y3, far2, own_b_normed = lax.optimization_barrier((y3, far2, own_b_normed))

    y4 = around(y3, None)
    far_a = jnp.concatenate([mirrored, far1, far2, far3])
    far_b = send(far_a, CORE)
    sets = (own_a_normed, normalize(far_a, place), own_b_normed, normalize(far_b, place))
    normed, resid = zip(*sets)
    acc = jnp.zeros((16 * slot_rows, vlm_weight.shape[0]), f32)
    kv_weights = []

    def add(e, own, near, after, acc):
        first = near[0].shape[0] // half - 2
        pieces = [(own, 0), (own, 1), (near[0], first), (near[0], first + 1)]
        pieces += [(after[0], 0), (after[1], 0), (near[1], first), (near[1], first + 1)]
        kvw, *rest = layer(place, normed, pieces, resid, acc, e, e == 3)
        kv_weights.append(kvw)
        return rest

    (acc,) = add(0, block, y0, y1, acc)
    (acc,) = add(1, z1, y1, y2, acc)
    (acc,) = add(2, z2, y2, y3, acc)
    feature, featt = add(3, z3, y3, y4, acc)

    part_b = project(feature, 1, kv_weights, bf16)
    swapped = send(part_b, CORE)
    part_a = project(feature, 0, kv_weights, f32)
    both = (part_a + swapped.astype(f32)).reshape(2, 4, slot_rows, 2 * width_act)
    mine = both[:, 0]
    for e in (1, 2, 3):
        mine = mine + send(both[:, e].astype(bf16), ALONG_X[e]).astype(f32)
    mine, featt = lax.optimization_barrier((mine, featt))
    other = send(mine[1].astype(bf16), MIRROR)
    feat1, feat3 = send(featt, ALONG_Y[1]), send(featt, ALONG_Y[3])
    other, feat1, feat3, featt = lax.optimization_barrier((other, feat1, feat3, featt))

    context, grads = attention(
        mine[0], other, queries, images, lengths, context_grad[0], place
    )

    by_y = jnp.stack([grads[0]] + [send(grads[e], ALONG_Y[e]) for e in (1, 2, 3)])
    by_y, featt = lax.optimization_barrier((by_y, featt))
    far, feat2 = send(by_y, MIRROR), send(featt, ALONG_Y[2])
    far, feat2 = lax.optimization_barrier((far, feat2))
    featt_all = jnp.stack([featt, feat1, feat2, feat3])
    grads_a = gather_along(jnp.stack([by_y, far]), ALONG_X)
    grads_b = send(grads_a, CORE)
    kv_weight_grad, sums = weight_grad(grads_a, grads_b, featt_all, place)
    for e in (1, 2, 3):
        kv_weight_grad = kv_weight_grad + send(sums[e], ALONG_Z[e]).astype(f32)
    return (context[None], kv_weight_grad)


def solution(mesh):
    in_specs = (
        P(("dp", "fsdp"), None, None),
        P(("dp", "fsdp")),
        P(("dp", "fsdp"), None, None),
        P(("dp", "fsdp")),
        P("dp", "fsdp"),
        P("fsdp", "dp"),
        P(),
        P(("dp", "fsdp"), None, None),
    )
    out_specs = (P(("dp", "fsdp"), None, None), P("fsdp", "dp"))
    return jax.shard_map(
        on_device, mesh=mesh, in_specs=in_specs, out_specs=out_specs, check_vma=False
    )
```

```python
import functools

import jax
import jax.numpy as jnp
from jax import lax
from jax.experimental import pallas as pl
from jax.experimental.pallas import tpu as pltpu
from jax.sharding import PartitionSpec as P

HEAD_DIM = 48
IMG_TOK = 16
ACT = 16
AXES = ("dp", "fsdp")

eps = 1e-06
masked_value = -1e30
bf16 = jnp.bfloat16
f32 = jnp.float32
MIB = 1024 * 1024


def pairs(step):
    table = []
    for i in range(256):
        h, x, c, l, y = step(i >> 7, (i >> 5) & 3, (i >> 4) & 1, (i >> 2) & 3, i & 3)
        table.append((i, h << 7 | x << 5 | c << 4 | l << 2 | y))
    return table


CORE = pairs(lambda h, x, c, l, y: (h, x, c ^ 1, l, y))
MIRROR = pairs(lambda h, x, c, l, y: (h ^ 1, x, c, l ^ 3, y))
HALF = pairs(lambda h, x, c, l, y: (h ^ 1, x, c, l, y))
ALONG_X = [pairs(lambda h, x, c, l, y, e=e: (h, x ^ e, c, l, y)) for e in range(4)]
ALONG_Y = [pairs(lambda h, x, c, l, y, e=e: (h, x, c, l, y ^ e)) for e in range(4)]
ALONG_Z = [pairs(lambda h, x, c, l, y, e=e: (h, x, c, l ^ e, y)) for e in range(4)]


def send(array, table):
    return lax.ppermute(array, AXES, table)


def gather_along(own, tables):
    return jnp.stack([own] + [send(own, tables[e]) for e in (1, 2, 3)])


def params(mib):
    return pltpu.CompilerParams(vmem_limit_bytes=mib * MIB)


def norm_kernel(place_ref, rows_ref, normed_ref, resid_ref):
    depth, chunk = resid_ref.shape[1], 16

    def step(i, carry):
        at = pl.ds(pl.multiple_of(i * chunk, chunk), chunk)
        widened = rows_ref[at].astype(f32)
        mean = jnp.mean(widened * widened, axis=-1, keepdims=True)
        normed_ref[at] = (widened * lax.rsqrt(mean + eps)).astype(bf16)
        return carry

    lax.fori_loop(0, rows_ref.shape[0] // chunk, step, 0)
    column = pl.multiple_of(place_ref[0] // 2 * (2 * depth), 128)
    both = rows_ref[:, pl.ds(column, 2 * depth)]
    resid_ref[...] = jnp.where(place_ref[0] % 2 == 0, both[:, :depth], both[:, depth:])


def normalize(rows, place):
    height, width = rows.shape
    depth, per = width // 16, 64
    return pl.pallas_call(
        norm_kernel,
        grid=(height // per,),
        in_specs=[
            pl.BlockSpec(memory_space=pltpu.SMEM),
            pl.BlockSpec((per, width), lambda i: (i, 0)),
        ],
        out_specs=[
            pl.BlockSpec((per, width), lambda i: (i, 0)),
            pl.BlockSpec((per, depth), lambda i: (i, 0)),
        ],
        out_shape=[
            jax.ShapeDtypeStruct((height, width), bf16),
            jax.ShapeDtypeStruct((height, depth), bf16),
        ],
        compiler_params=params(12),
        name="norm",
    )(place, rows)


def layer_kernel(place_ref, *refs, finish):
    normed_refs, piece_refs = refs[:4], refs[4:12]
    resid_refs, acc_ref = refs[12:16], refs[16]
    kvw_ref, *out_refs, weights = refs[17:]
    y = place_ref[2]
    out = acc_ref.shape[1]
    half = piece_refs[0].shape[0]
    depth = 2 * half
    for i, ref in enumerate(piece_refs):
        at = pl.multiple_of((y ^ (i // 2)) * depth + i % 2 * half, 32)
        weights[pl.ds(at, half)] = ref[...]
    kvw_ref[...] = jnp.concatenate(
        [weights[f * depth : (f + 1) * depth, out:] for f in range(4)], axis=1
    )
    normed = jnp.concatenate([ref[...] for ref in normed_refs], axis=0)
    total = acc_ref[...] + jnp.dot(normed, weights[:, :out], preferred_element_type=f32)
    if finish:
        feature_ref, featt_ref = out_refs
        resid = jnp.concatenate([ref[...] for ref in resid_refs], axis=0).astype(f32)
        feature = (resid + total / (1.0 + jnp.exp(-total))).astype(bf16)
        feature_ref[...] = feature
        featt_ref[...] = feature.T
    else:
        out_refs[0][...] = total


def layer(place, normed, pieces, resid, acc, e, finish):
    rows, out = acc.shape
    wide = pieces[0][0].shape[1]
    kv = wide - out
    depth = normed[0].shape[1] // 16
    half = depth // 2

    def whole(shape):
        return pl.BlockSpec(shape, lambda i, place: (0, 0))

    if finish:
        shapes = [((rows, out), bf16), ((out, rows), bf16)]
    else:
        shapes = [((rows, out), f32)]
    shapes = [((depth, 4 * kv), bf16)] + shapes
    return pl.pallas_call(
        functools.partial(layer_kernel, finish=finish),
        grid_spec=pltpu.PrefetchScalarGridSpec(
            num_scalar_prefetch=1,
            grid=(1,),
            in_specs=[
                pl.BlockSpec((rows // 4, 4 * depth), lambda i, place: (0, place[1] ^ e)),
            ]
            * 4
            + [
                pl.BlockSpec((half, wide), lambda i, place, at=at: (at, 0)) for _, at in pieces
            ]
            + [whole(r.shape) for r in resid]
            + [whole(acc.shape)],
            out_specs=[whole(shape) for shape, _ in shapes],
            scratch_shapes=[pltpu.VMEM((4 * depth, wide), bf16)],
        ),
        out_shape=[jax.ShapeDtypeStruct(shape, dtype) for shape, dtype in shapes],
        compiler_params=params(24),
        name="layer",
    )(place, *normed, *[array for array, _ in pieces], *resid, acc)


def project_kernel(feature_ref, *refs):
    out_ref = refs[-1]
    kv = refs[0].shape[1]
    for e, w_ref in enumerate(refs[:-1]):
        out_ref[:, e * kv : (e + 1) * kv] = jnp.dot(
            feature_ref[...], w_ref[...], preferred_element_type=f32
        ).astype(out_ref.dtype)


def project(feature, half, weights, dtype):
    rows, depth = feature.shape[0] // 2, feature.shape[1]
    kv = weights[0].shape[1]
    return pl.pallas_call(
        project_kernel,
        grid=(1,),
        in_specs=[pl.BlockSpec((rows, depth), lambda i: (half, 0))]
        + [pl.BlockSpec((depth, kv), lambda i: (0, 0))] * 4,
        out_specs=pl.BlockSpec((rows, 4 * kv), lambda i: (0, 0)),
        out_shape=jax.ShapeDtypeStruct((rows, 4 * kv), dtype),
        compiler_params=params(16),
        name="project",
    )(feature, *weights)


def attention_kernel(
    place_ref, images_ref, lengths_ref, own_ref, other_ref, q_ref, cg_ref, context_ref, grads_ref, kvs
):
    key_rows, width = own_ref.shape
    width_act = width // 2
    qrows = q_ref.shape[0]
    heads = 8
    cols = heads * HEAD_DIM
    scale = HEAD_DIM ** (-0.5)
    piece = width // 16
    l, y = place_ref[1], place_ref[2]
    last = (((1,), (1,)), ((), ()))
    first = (((0,), (0,)), ((), ()))
    wide = width // 4
    for e in range(4):
        own = own_ref[:, e * wide : (e + 1) * wide]
        other = other_ref[:, (3 - e) * wide : (4 - e) * wide].astype(f32)
        kvs[e] = (own + other).astype(bf16)
    row_head = lax.broadcasted_iota(jnp.int32, (heads * key_rows, cols), 0) // key_rows
    col_head = lax.broadcasted_iota(jnp.int32, (heads * key_rows, cols), 1) // HEAD_DIM
    same = row_head == col_head
    key_live = (
        lax.broadcasted_iota(jnp.int32, (heads, key_rows, qrows), 1) < images_ref[0] * IMG_TOK
    )
    query_live = lax.broadcasted_iota(jnp.int32, (qrows, cols), 0) % ACT < lengths_ref[0]

    def by_head(flat):
        return flat.reshape(heads, key_rows, qrows)

    def spread(rows):
        return jnp.where(same, jnp.concatenate([rows] * heads, axis=0), jnp.zeros((), bf16))

    def collapse(big):
        return jnp.sum(jnp.where(same, big, 0.0).reshape(heads, key_rows, cols), axis=0)

    for g in range(width_act // cols):
        at = slice(g * cols, (g + 1) * cols)
        column = slice(g % 2 * cols, (g % 2 + 1) * cols)
        keys = spread(kvs[(g // 2) ^ l, :, column])
        values = spread(kvs[(2 + g // 2) ^ l, :, column])
        queries = q_ref[:, at]
        grad_in = jnp.where(query_live, cg_ref[:, at], jnp.zeros((), bf16))
        scores = by_head(lax.dot_general(keys, queries, last, preferred_element_type=f32) * scale)
        scores = jnp.where(key_live, scores, masked_value)
        exponent = jnp.exp(scores - jnp.max(scores, axis=1, keepdims=True))
        probs = exponent / jnp.sum(exponent, axis=1, keepdims=True)
        probs_low = probs.astype(bf16).reshape(heads * key_rows, qrows)
        mixed = lax.dot_general(probs_low, values, first, preferred_element_type=f32)
        context_ref[:, at] = jnp.where(query_live, mixed, 0.0).astype(bf16)
        prob_grad = by_head(lax.dot_general(values, grad_in, last, preferred_element_type=f32))
        centre = jnp.sum(prob_grad * probs, axis=1, keepdims=True)
        score_grad = (probs * (prob_grad - centre)).astype(bf16).reshape(heads * key_rows, qrows)
        value_grad = collapse(jnp.dot(probs_low, grad_in, preferred_element_type=f32)).astype(bf16)
        key_grad = jnp.dot(score_grad, queries, preferred_element_type=f32)
        key_grad = (collapse(key_grad) * scale).astype(bf16)
        per = cols // piece
        for start, grad in ((g * per, key_grad), (width_act // piece + g * per, value_grad)):
            for j in range(per):
                f = start + j
                column = f // 4 * piece
                grads_ref[(f % 4) ^ y, :, column : column + piece] = grad[
                    :, j * piece : (j + 1) * piece
                ]


def attention(own, other, queries, images, lengths, context_grad, place):
    key_rows, width = own.shape
    smem, vmem = pl.BlockSpec(memory_space=pltpu.SMEM), pl.BlockSpec(memory_space=pltpu.VMEM)
    return pl.pallas_call(
        attention_kernel,
        in_specs=[smem, smem, smem, vmem, vmem, vmem, vmem],
        out_specs=[vmem, vmem],
        out_shape=[
            jax.ShapeDtypeStruct(queries.shape, bf16),
            jax.ShapeDtypeStruct((4, key_rows, width // 4), bf16),
        ],
        scratch_shapes=[pltpu.VMEM((4, key_rows, width // 4), bf16)],
        compiler_params=params(24),
        name="attention",
    )(place, images, lengths, own, other, queries, context_grad)


def weight_grad_kernel(place_ref, a_ref, b_ref, featt_ref, own_ref, sends_ref, acc):
    step = pl.program_id(0)
    l, y = place_ref[1], place_ref[2]
    wide = acc.shape[1]
    packed = [ref[:, m, 0] for ref in (a_ref, b_ref) for m in range(2)]
    grads = jnp.concatenate(packed, axis=0).reshape(-1, wide)
    term = jnp.dot(featt_ref[0], grads, preferred_element_type=f32)

    @pl.when(step == 0)
    def _():
        acc[...] = term

    @pl.when(step > 0)
    def _():
        acc[...] += term

    @pl.when(step == pl.num_programs(0) - 1)
    def _():
        total = acc[...].T
        kv = wide // 4
        for fl in range(4):
            block = total[fl * kv : (fl + 1) * kv]
            sends_ref[fl ^ l] = block.astype(bf16)

            @pl.when(l == fl)
            def _():
                own_ref[...] = block


def weight_grad(grads_a, grads_b, featt, place):
    blocks, out, rows = featt.shape
    key_rows, wide = grads_a.shape[-2:]
    kv = wide // 4
    near = pl.BlockSpec((4, 2, 1, key_rows, wide), lambda i, place: (0, 0, i, 0, 0))
    return pl.pallas_call(
        weight_grad_kernel,
        grid_spec=pltpu.PrefetchScalarGridSpec(
            num_scalar_prefetch=1,
            grid=(blocks,),
            in_specs=[
                near,
                near,
                pl.BlockSpec((1, out, rows), lambda i, place: (i, 0, 0)),
            ],
            out_specs=[
                pl.BlockSpec((kv, out), lambda i, place: (0, 0)),
                pl.BlockSpec((4, kv, out), lambda i, place: (0, 0, 0)),
            ],
            scratch_shapes=[pltpu.VMEM((out, wide), f32)],
        ),
        out_shape=[
            jax.ShapeDtypeStruct((kv, out), f32),
            jax.ShapeDtypeStruct((4, kv, out), bf16),
        ],
        compiler_params=params(16),
        name="weight_grad",
    )(place, grads_a, grads_b, featt)


def on_device(
    vlm_rows, images, action_hidden, lengths, vlm_weight, kv_weight, query_weight, context_grad
):
    _, slot_rows, width = vlm_rows.shape
    width_act = query_weight.shape[0]
    dp, fsdp = lax.axis_index("dp"), lax.axis_index("fsdp")
    place = jnp.stack([dp, fsdp // 4, fsdp % 4]).astype(jnp.int32)

    block = jnp.concatenate([vlm_weight.T, kv_weight.T], axis=1)
    half = block.shape[0] // 2

    def around(before, w):
        up, down = before
        low, high = down[-2 * half : -half], up[-half:]
        if w is not None:
            low, high = jnp.concatenate([low, w]), jnp.concatenate([high, w])
        return send(low, ALONG_Y[1]), send(high, ALONG_Y[3])

    def along_x(rows, e):
        return send(rows, ALONG_X[e])

    rows = vlm_rows[0]
    y0 = send(block, ALONG_Y[1]), send(block, ALONG_Y[3])
    z1, own1, own3 = send(block, ALONG_Z[1]), along_x(rows, 1), along_x(rows, 3)
    y0, z1, own1, own3, block, rows = lax.optimization_barrier(
        (y0, z1, own1, own3, block, rows)
    )

    y1, z2 = around(y0, z1), send(block, ALONG_Z[2])
    mirrored, own2 = send(rows, MIRROR), along_x(rows, 2)
    y1, z2, mirrored, own2 = lax.optimization_barrier((y1, z2, mirrored, own2))

    y2, z3 = around(y1, z2), send(z2, ALONG_Z[1])
    far1, far3 = along_x(mirrored, 1), along_x(mirrored, 3)
    own_a = jnp.concatenate([rows, own1, own2, own3])
    queries = lax.dot_general(
        action_hidden[0], query_weight, (((1,), (1,)), ((), ())), preferred_element_type=f32
    ).astype(bf16)
    own_a_normed = normalize(own_a, place)
    y2, z3, far1, far3, mirrored, queries, own_a, own_a_normed = lax.optimization_barrier(
        (y2, z3, far1, far3, mirrored, queries, own_a, own_a_normed)
    )

    y3, far2 = around(y2, z3), along_x(mirrored, 2)
    own_b = send(own_a, CORE)
    own_b_normed = normalize(own_b, place)
    y3, far2, own_b_normed = lax.optimization_barrier((y3, far2, own_b_normed))

    y4 = around(y3, None)
    far_a = jnp.concatenate([mirrored, far1, far2, far3])
    far_b = send(far_a, CORE)
    sets = (own_a_normed, normalize(far_a, place), own_b_normed, normalize(far_b, place))
    normed, resid = zip(*sets)
    acc = jnp.zeros((16 * slot_rows, vlm_weight.shape[0]), f32)
    kv_weights = []

    def add(e, own, near, after, acc):
        first = near[0].shape[0] // half - 2
        pieces = [(own, 0), (own, 1), (near[0], first), (near[0], first + 1)]
        pieces += [(after[0], 0), (after[1], 0), (near[1], first), (near[1], first + 1)]
        kvw, *rest = layer(place, normed, pieces, resid, acc, e, e == 3)
        kv_weights.append(kvw)
        return rest

    (acc,) = add(0, block, y0, y1, acc)
    (acc,) = add(1, z1, y1, y2, acc)
    (acc,) = add(2, z2, y2, y3, acc)
    feature, featt = add(3, z3, y3, y4, acc)

    part_b = project(feature, 1, kv_weights, bf16)
    swapped = send(part_b, CORE)
    part_a = project(feature, 0, kv_weights, f32)
    both = (part_a + swapped.astype(f32)).reshape(2, 4, slot_rows, 2 * width_act)
    mine = both[:, 0]
    for e in (1, 2, 3):
        mine = mine + send(both[:, e].astype(bf16), ALONG_X[e]).astype(f32)
    mine, featt = lax.optimization_barrier((mine, featt))
    other = send(mine[1].astype(bf16), MIRROR)
    feat1, feat3 = send(featt, ALONG_Y[1]), send(featt, ALONG_Y[3])
    other, feat1, feat3, featt = lax.optimization_barrier((other, feat1, feat3, featt))

    context, grads = attention(
        mine[0], other, queries, images, lengths, context_grad[0], place
    )

    by_y = jnp.stack([grads[0]] + [send(grads[e], ALONG_Y[e]) for e in (1, 2, 3)])
    by_y, featt = lax.optimization_barrier((by_y, featt))
    far, feat2 = send(by_y, MIRROR), send(featt, ALONG_Y[2])
    far, feat2 = lax.optimization_barrier((far, feat2))
    featt_all = jnp.stack([featt, feat1, feat2, feat3])
    grads_a = gather_along(jnp.stack([by_y, far]), ALONG_X)
    grads_b = send(grads_a, CORE)
    kv_weight_grad, sums = weight_grad(grads_a, grads_b, featt_all, place)
    for e in (1, 2, 3):
        kv_weight_grad = kv_weight_grad + send(sums[e], ALONG_Z[e]).astype(f32)
    return (context[None], kv_weight_grad)


def solution(mesh):
    in_specs = (
        P(("dp", "fsdp"), None, None),
        P(("dp", "fsdp")),
        P(("dp", "fsdp"), None, None),
        P(("dp", "fsdp")),
        P("dp", "fsdp"),
        P("fsdp", "dp"),
        P(),
        P(("dp", "fsdp"), None, None),
    )
    out_specs = (P(("dp", "fsdp"), None, None), P("fsdp", "dp"))
    return jax.shard_map(
        on_device, mesh=mesh, in_specs=in_specs, out_specs=out_specs, check_vma=False
    )
```

```python
import functools

import jax
import jax.numpy as jnp
from jax import lax
from jax.experimental import pallas as pl
from jax.experimental.pallas import tpu as pltpu
from jax.sharding import PartitionSpec as P

HEAD_DIM = 48
IMG_TOK = 16
ACT = 16
AXES = ("dp", "fsdp")

eps = 1e-06
masked_value = -1e30
bf16 = jnp.bfloat16
f32 = jnp.float32
MIB = 1024 * 1024


def pairs(step):
    table = []
    for i in range(256):
        h, x, c, l, y = step(i >> 7, (i >> 5) & 3, (i >> 4) & 1, (i >> 2) & 3, i & 3)
        table.append((i, h << 7 | x << 5 | c << 4 | l << 2 | y))
    return table


CORE = pairs(lambda h, x, c, l, y: (h, x, c ^ 1, l, y))
MIRROR = pairs(lambda h, x, c, l, y: (h ^ 1, x, c, l ^ 3, y))
HALF = pairs(lambda h, x, c, l, y: (h ^ 1, x, c, l, y))
ALONG_X = [pairs(lambda h, x, c, l, y, e=e: (h, x ^ e, c, l, y)) for e in range(4)]
ALONG_Y = [pairs(lambda h, x, c, l, y, e=e: (h, x, c, l, y ^ e)) for e in range(4)]
ALONG_Z = [pairs(lambda h, x, c, l, y, e=e: (h, x, c, l ^ e, y)) for e in range(4)]


def send(array, table):
    return lax.ppermute(array, AXES, table)


def gather_along(own, tables):
    return jnp.stack([own] + [send(own, tables[e]) for e in (1, 2, 3)])


def params(mib):
    return pltpu.CompilerParams(vmem_limit_bytes=mib * MIB)


def norm_kernel(place_ref, rows_ref, normed_ref, resid_ref):
    depth, chunk = resid_ref.shape[1], 16

    def step(i, carry):
        at = pl.ds(pl.multiple_of(i * chunk, chunk), chunk)
        widened = rows_ref[at].astype(f32)
        mean = jnp.mean(widened * widened, axis=-1, keepdims=True)
        normed_ref[at] = (widened * lax.rsqrt(mean + eps)).astype(bf16)
        return carry

    lax.fori_loop(0, rows_ref.shape[0] // chunk, step, 0)
    column = pl.multiple_of(place_ref[0] // 2 * (2 * depth), 128)
    both = rows_ref[:, pl.ds(column, 2 * depth)]
    resid_ref[...] = jnp.where(place_ref[0] % 2 == 0, both[:, :depth], both[:, depth:])


def normalize(rows, place):
    height, width = rows.shape
    depth, per = width // 16, 64
    return pl.pallas_call(
        norm_kernel,
        grid=(height // per,),
        in_specs=[
            pl.BlockSpec(memory_space=pltpu.SMEM),
            pl.BlockSpec((per, width), lambda i: (i, 0)),
        ],
        out_specs=[
            pl.BlockSpec((per, width), lambda i: (i, 0)),
            pl.BlockSpec((per, depth), lambda i: (i, 0)),
        ],
        out_shape=[
            jax.ShapeDtypeStruct((height, width), bf16),
            jax.ShapeDtypeStruct((height, depth), bf16),
        ],
        compiler_params=params(12),
        name="norm",
    )(place, rows)


def layer_kernel(place_ref, *refs, finish):
    normed_refs, piece_refs = refs[:4], refs[4:12]
    resid_refs, acc_ref = refs[12:16], refs[16]
    kvw_ref, *out_refs, weights = refs[17:]
    y = place_ref[2]
    out = acc_ref.shape[1]
    half = piece_refs[0].shape[0]
    depth = 2 * half
    for i, ref in enumerate(piece_refs):
        at = pl.multiple_of((y ^ (i // 2)) * depth + i % 2 * half, 32)
        weights[pl.ds(at, half)] = ref[...]
    kvw_ref[...] = jnp.concatenate(
        [weights[f * depth : (f + 1) * depth, out:] for f in range(4)], axis=1
    )
    normed = jnp.concatenate([ref[...] for ref in normed_refs], axis=0)
    total = acc_ref[...] + jnp.dot(normed, weights[:, :out], preferred_element_type=f32)
    if finish:
        feature_ref, featt_ref = out_refs
        resid = jnp.concatenate([ref[...] for ref in resid_refs], axis=0).astype(f32)
        feature = (resid + total / (1.0 + jnp.exp(-total))).astype(bf16)
        feature_ref[...] = feature
        featt_ref[...] = feature.T
    else:
        out_refs[0][...] = total


def layer(place, normed, pieces, resid, acc, e, finish):
    rows, out = acc.shape
    wide = pieces[0][0].shape[1]
    kv = wide - out
    depth = normed[0].shape[1] // 16
    half = depth // 2

    def whole(shape):
        return pl.BlockSpec(shape, lambda i, place: (0, 0))

    if finish:
        shapes = [((rows, out), bf16), ((out, rows), bf16)]
    else:
        shapes = [((rows, out), f32)]
    shapes = [((depth, 4 * kv), bf16)] + shapes
    return pl.pallas_call(
        functools.partial(layer_kernel, finish=finish),
        grid_spec=pltpu.PrefetchScalarGridSpec(
            num_scalar_prefetch=1,
            grid=(1,),
            in_specs=[
                pl.BlockSpec((rows // 4, 4 * depth), lambda i, place: (0, place[1] ^ e)),
            ]
            * 4
            + [
                pl.BlockSpec((half, wide), lambda i, place, at=at: (at, 0)) for _, at in pieces
            ]
            + [whole(r.shape) for r in resid]
            + [whole(acc.shape)],
            out_specs=[whole(shape) for shape, _ in shapes],
            scratch_shapes=[pltpu.VMEM((4 * depth, wide), bf16)],
        ),
        out_shape=[jax.ShapeDtypeStruct(shape, dtype) for shape, dtype in shapes],
        compiler_params=params(24),
        name="layer",
    )(place, *normed, *[array for array, _ in pieces], *resid, acc)


def project_kernel(feature_ref, *refs):
    out_ref = refs[-1]
    kv = refs[0].shape[1]
    for e, w_ref in enumerate(refs[:-1]):
        out_ref[:, e * kv : (e + 1) * kv] = jnp.dot(
            feature_ref[...], w_ref[...], preferred_element_type=f32
        ).astype(out_ref.dtype)


def project(feature, half, weights, dtype):
    rows, depth = feature.shape[0] // 2, feature.shape[1]
    kv = weights[0].shape[1]
    return pl.pallas_call(
        project_kernel,
        grid=(1,),
        in_specs=[pl.BlockSpec((rows, depth), lambda i: (half, 0))]
        + [pl.BlockSpec((depth, kv), lambda i: (0, 0))] * 4,
        out_specs=pl.BlockSpec((rows, 4 * kv), lambda i: (0, 0)),
        out_shape=jax.ShapeDtypeStruct((rows, 4 * kv), dtype),
        compiler_params=params(16),
        name="project",
    )(feature, *weights)


def attention_kernel(
    place_ref, images_ref, lengths_ref, own_ref, other_ref, q_ref, cg_ref, context_ref, grads_ref, kvs
):
    key_rows, width = own_ref.shape
    width_act = width // 2
    qrows = q_ref.shape[0]
    heads = 8
    cols = heads * HEAD_DIM
    scale = HEAD_DIM ** (-0.5)
    piece = width // 16
    l, y = place_ref[1], place_ref[2]
    last = (((1,), (1,)), ((), ()))
    first = (((0,), (0,)), ((), ()))
    wide = width // 4
    for e in range(4):
        own = own_ref[:, e * wide : (e + 1) * wide]
        other = other_ref[:, (3 - e) * wide : (4 - e) * wide].astype(f32)
        kvs[e] = (own + other).astype(bf16)
    row_head = lax.broadcasted_iota(jnp.int32, (heads * key_rows, cols), 0) // key_rows
    col_head = lax.broadcasted_iota(jnp.int32, (heads * key_rows, cols), 1) // HEAD_DIM
    same = row_head == col_head
    key_live = (
        lax.broadcasted_iota(jnp.int32, (heads, key_rows, qrows), 1) < images_ref[0] * IMG_TOK
    )
    query_live = lax.broadcasted_iota(jnp.int32, (qrows, cols), 0) % ACT < lengths_ref[0]

    def by_head(flat):
        return flat.reshape(heads, key_rows, qrows)

    def spread(rows):
        return jnp.where(same, jnp.concatenate([rows] * heads, axis=0), jnp.zeros((), bf16))

    def collapse(big):
        return jnp.sum(jnp.where(same, big, 0.0).reshape(heads, key_rows, cols), axis=0)

    for g in range(width_act // cols):
        at = slice(g * cols, (g + 1) * cols)
        column = slice(g % 2 * cols, (g % 2 + 1) * cols)
        keys = spread(kvs[(g // 2) ^ l, :, column])
        values = spread(kvs[(2 + g // 2) ^ l, :, column])
        queries = q_ref[:, at]
        grad_in = jnp.where(query_live, cg_ref[:, at], jnp.zeros((), bf16))
        scores = by_head(lax.dot_general(keys, queries, last, preferred_element_type=f32) * scale)
        scores = jnp.where(key_live, scores, masked_value)
        exponent = jnp.exp(scores - jnp.max(scores, axis=1, keepdims=True))
        probs = exponent / jnp.sum(exponent, axis=1, keepdims=True)
        probs_low = probs.astype(bf16).reshape(heads * key_rows, qrows)
        mixed = lax.dot_general(probs_low, values, first, preferred_element_type=f32)
        context_ref[:, at] = jnp.where(query_live, mixed, 0.0).astype(bf16)
        prob_grad = by_head(lax.dot_general(values, grad_in, last, preferred_element_type=f32))
        centre = jnp.sum(prob_grad * probs, axis=1, keepdims=True)
        score_grad = (probs * (prob_grad - centre)).astype(bf16).reshape(heads * key_rows, qrows)
        value_grad = collapse(jnp.dot(probs_low, grad_in, preferred_element_type=f32)).astype(bf16)
        key_grad = jnp.dot(score_grad, queries, preferred_element_type=f32)
        key_grad = (collapse(key_grad) * scale).astype(bf16)
        per = cols // piece
        for start, grad in ((g * per, key_grad), (width_act // piece + g * per, value_grad)):
            for j in range(per):
                f = start + j
                column = f // 4 * piece
                grads_ref[(f % 4) ^ y, :, column : column + piece] = grad[
                    :, j * piece : (j + 1) * piece
                ]


def attention(own, other, queries, images, lengths, context_grad, place):
    key_rows, width = own.shape
    smem, vmem = pl.BlockSpec(memory_space=pltpu.SMEM), pl.BlockSpec(memory_space=pltpu.VMEM)
    return pl.pallas_call(
        attention_kernel,
        in_specs=[smem, smem, smem, vmem, vmem, vmem, vmem],
        out_specs=[vmem, vmem],
        out_shape=[
            jax.ShapeDtypeStruct(queries.shape, bf16),
            jax.ShapeDtypeStruct((4, key_rows, width // 4), bf16),
        ],
        scratch_shapes=[pltpu.VMEM((4, key_rows, width // 4), bf16)],
        compiler_params=params(24),
        name="attention",
    )(place, images, lengths, own, other, queries, context_grad)


def weight_grad_kernel(place_ref, a_ref, b_ref, featt_ref, own_ref, sends_ref, acc):
    step = pl.program_id(0)
    l, y = place_ref[1], place_ref[2]
    wide = acc.shape[1]
    packed = [ref[:, m, 0] for ref in (a_ref, b_ref) for m in range(2)]
    grads = jnp.concatenate(packed, axis=0).reshape(-1, wide)
    term = jnp.dot(featt_ref[0], grads, preferred_element_type=f32)

    @pl.when(step == 0)
    def _():
        acc[...] = term

    @pl.when(step > 0)
    def _():
        acc[...] += term

    @pl.when(step == pl.num_programs(0) - 1)
    def _():
        total = acc[...].T
        kv = wide // 4
        for fl in range(4):
            block = total[fl * kv : (fl + 1) * kv]
            sends_ref[fl ^ l] = block.astype(bf16)

            @pl.when(l == fl)
            def _():
                own_ref[...] = block


def weight_grad(grads_a, grads_b, featt, place):
    blocks, out, rows = featt.shape
    key_rows, wide = grads_a.shape[-2:]
    kv = wide // 4
    near = pl.BlockSpec((4, 2, 1, key_rows, wide), lambda i, place: (0, 0, i, 0, 0))
    return pl.pallas_call(
        weight_grad_kernel,
        grid_spec=pltpu.PrefetchScalarGridSpec(
            num_scalar_prefetch=1,
            grid=(blocks,),
            in_specs=[
                near,
                near,
                pl.BlockSpec((1, out, rows), lambda i, place: (i, 0, 0)),
            ],
            out_specs=[
                pl.BlockSpec((kv, out), lambda i, place: (0, 0)),
                pl.BlockSpec((4, kv, out), lambda i, place: (0, 0, 0)),
            ],
            scratch_shapes=[pltpu.VMEM((out, wide), f32)],
        ),
        out_shape=[
            jax.ShapeDtypeStruct((kv, out), f32),
            jax.ShapeDtypeStruct((4, kv, out), bf16),
        ],
        compiler_params=params(16),
        name="weight_grad",
    )(place, grads_a, grads_b, featt)


def on_device(
    vlm_rows, images, action_hidden, lengths, vlm_weight, kv_weight, query_weight, context_grad
):
    _, slot_rows, width = vlm_rows.shape
    width_act = query_weight.shape[0]
    dp, fsdp = lax.axis_index("dp"), lax.axis_index("fsdp")
    place = jnp.stack([dp, fsdp // 4, fsdp % 4]).astype(jnp.int32)

    block = jnp.concatenate([vlm_weight.T, kv_weight.T], axis=1)
    half = block.shape[0] // 2

    def around(before, w):
        up, down = before
        low, high = down[-2 * half : -half], up[-half:]
        if w is not None:
            low, high = jnp.concatenate([low, w]), jnp.concatenate([high, w])
        return send(low, ALONG_Y[1]), send(high, ALONG_Y[3])

    def along_x(rows, e):
        return send(rows, ALONG_X[e])

    rows = vlm_rows[0]
    y0 = send(block, ALONG_Y[1]), send(block, ALONG_Y[3])
    z1, own1, own3 = send(block, ALONG_Z[1]), along_x(rows, 1), along_x(rows, 3)
    y0, z1, own1, own3, block, rows = lax.optimization_barrier(
        (y0, z1, own1, own3, block, rows)
    )

    y1, z2 = around(y0, z1), send(z1, ALONG_Z[3])
    mirrored, own2 = send(rows, MIRROR), along_x(rows, 2)
    y1, z2, mirrored, own2 = lax.optimization_barrier((y1, z2, mirrored, own2))

    y2, z3 = around(y1, z2), send(z2, ALONG_Z[1])
    far1, far3 = along_x(mirrored, 1), along_x(mirrored, 3)
    own_a = jnp.concatenate([rows, own1, own2, own3])
    queries = lax.dot_general(
        action_hidden[0], query_weight, (((1,), (1,)), ((), ())), preferred_element_type=f32
    ).astype(bf16)
    own_a_normed = normalize(own_a, place)
    y2, z3, far1, far3, mirrored, queries, own_a, own_a_normed = lax.optimization_barrier(
        (y2, z3, far1, far3, mirrored, queries, own_a, own_a_normed)
    )

    y3, far2 = around(y2, z3), along_x(mirrored, 2)
    own_b = send(own_a, CORE)
    own_b_normed = normalize(own_b, place)
    y3, own_b_normed = lax.optimization_barrier((y3, own_b_normed))

    y4 = around(y3, None)
    far_a = jnp.concatenate([mirrored, far1, far2, far3])
    far_b = send(far_a, CORE)
    sets = (own_a_normed, normalize(far_a, place), own_b_normed, normalize(far_b, place))
    normed, resid = zip(*sets)
    acc = jnp.zeros((16 * slot_rows, vlm_weight.shape[0]), f32)
    kv_weights = []

    def add(e, own, near, after, acc):
        first = near[0].shape[0] // half - 2
        pieces = [(own, 0), (own, 1), (near[0], first), (near[0], first + 1)]
        pieces += [(after[0], 0), (after[1], 0), (near[1], first), (near[1], first + 1)]
        kvw, *rest = layer(place, normed, pieces, resid, acc, e, e == 3)
        kv_weights.append(kvw)
        return rest

    (acc,) = add(0, block, y0, y1, acc)
    (acc,) = add(1, z1, y1, y2, acc)
    (acc,) = add(2, z2, y2, y3, acc)
    feature, featt = add(3, z3, y3, y4, acc)

    part_b = project(feature, 1, kv_weights, bf16)
    swapped = send(part_b, CORE)
    part_a = project(feature, 0, kv_weights, f32)
    both = (part_a + swapped.astype(f32)).reshape(2, 4, slot_rows, 2 * width_act)
    mine = both[:, 0]
    for e in (1, 2, 3):
        mine = mine + send(both[:, e].astype(bf16), ALONG_X[e]).astype(f32)
    mine, featt = lax.optimization_barrier((mine, featt))
    other = send(mine[1].astype(bf16), MIRROR)
    feat1, feat3 = send(featt, ALONG_Y[1]), send(featt, ALONG_Y[3])
    other, feat1, feat3, featt = lax.optimization_barrier((other, feat1, feat3, featt))

    context, grads = attention(
        mine[0], other, queries, images, lengths, context_grad[0], place
    )

    by_y = jnp.stack([grads[0]] + [send(grads[e], ALONG_Y[e]) for e in (1, 2, 3)])
    by_y, featt = lax.optimization_barrier((by_y, featt))
    far, feat2 = send(by_y, MIRROR), send(featt, ALONG_Y[2])
    far, feat2 = lax.optimization_barrier((far, feat2))
    featt_all = jnp.stack([featt, feat1, feat2, feat3])
    grads_a = gather_along(jnp.stack([by_y, far]), ALONG_X)
    grads_b = send(grads_a, CORE)
    kv_weight_grad, sums = weight_grad(grads_a, grads_b, featt_all, place)
    for e in (1, 2, 3):
        kv_weight_grad = kv_weight_grad + send(sums[e], ALONG_Z[e]).astype(f32)
    return (context[None], kv_weight_grad)


def solution(mesh):
    in_specs = (
        P(("dp", "fsdp"), None, None),
        P(("dp", "fsdp")),
        P(("dp", "fsdp"), None, None),
        P(("dp", "fsdp")),
        P("dp", "fsdp"),
        P("fsdp", "dp"),
        P(),
        P(("dp", "fsdp"), None, None),
    )
    out_specs = (P(("dp", "fsdp"), None, None), P("fsdp", "dp"))
    return jax.shard_map(
        on_device, mesh=mesh, in_specs=in_specs, out_specs=out_specs, check_vma=False
    )
```
